32 devices in a mesh: ctx: 16 (over z, x, core), chan: 2 (over y).
Axes of the slice: x: 2, y: 2, z: 4, core: 2. Of those that a mesh axis runs over, the one named last changes fastest.
Arguments:
- grad_out: bfloat16 [64, 16384], P('chan', 'ctx'), may hold values from -6 to 6
- query: bfloat16 [64, 16384], P('chan', 'ctx'), may hold values from -6 to 6
- key_proj: bfloat16 [64, 16384], P('chan', 'ctx'), may hold values from -6 to 6
- value: bfloat16 [64, 16384], P('chan', 'ctx'), may hold values from -6 to 6
- filter_param: float32 [32, 16384], P(None, 'ctx'), may hold values from -6 to 6
Outputs:
- grad_query: bfloat16 [64, 16384], P('chan', 'ctx')
- grad_key: bfloat16 [64, 16384], P('chan', 'ctx')
- grad_value: bfloat16 [64, 16384], P('chan', 'ctx')
- grad_filter: float32 [32, 16384], P(None, 'ctx')
The draws below stay inside these ranges and needn't reach their ends.
All inputs are finite; a program needn't handle non-finite values.
Results may differ from the reference program's by a relative error of at most 0.004.
Values sent between devices are 32-bit elements; how exact they have to be, the bound alone decides.
A program may use at most 128 MiB of HBM per device.

```python
import math
import jax
import jax.numpy as jnp

TOKENS = 16384
CHANNELS = 64
FILTERS = 32
N_CHAN = 2


def block_levels(own_key, extent, shards, least, high):
    gain, own = 1.0, jax.random.fold_in(own_key, 6)
    for dim, blocks in shards:
        steps = jnp.exp(jax.random.uniform(jax.random.fold_in(own, dim), (blocks,), jnp.float32, least / len(shards), high / len(shards)))
        gain = gain * jnp.repeat(steps, extent[dim] // blocks).reshape([-1 if axis == dim else 1 for axis in range(len(extent))])
    return gain


def normal_values(rng, shape, scale, reach, pieces=(), dtype=jnp.bfloat16):
    drawn = jax.random.normal(rng, shape, jnp.float32) * scale
    if len(pieces) > 0:
        drawn = block_levels(rng, shape, pieces, -0.22, 0.18) * drawn
    return jnp.clip(drawn, min=-reach, max=reach).astype(dtype)


def setup_inputs(seed: int = 0) -> dict:
    streams_of = jax.random.split(jax.random.key(seed), 6)
    grad_out = normal_values(streams_of[0], (CHANNELS, TOKENS), 1.0, 6.0, ((0, 2), (1, 16)))
    query = normal_values(streams_of[1], (CHANNELS, TOKENS), 1.0, 6.0, ((0, 2), (1, 16)))
    key_proj = normal_values(streams_of[2], (CHANNELS, TOKENS), 1.0, 6.0, ((0, 2), (1, 16)))
    value = normal_values(streams_of[3], (CHANNELS, TOKENS), 1.0, 6.0, ((0, 2), (1, 16)))
    filter_param = normal_values(streams_of[4], (FILTERS, TOKENS), 1.0, 6.0, ((1, 16),), jnp.float32)
    return {"grad_out": grad_out, "query": query, "key_proj": key_proj, "value": value, "filter_param": filter_param}


def reference(grad_out, query, key_proj, value, filter_param):
    filter_scale = 1.0 / math.sqrt(TOKENS)
    filt = filter_param.T * filter_scale
    padded = 2 * TOKENS
    filter_spec = jnp.fft.rfft(filt, n=padded, axis=0)
    dq_list = []
    dk_list = []
    dv_list = []
    filter_total = jnp.zeros((TOKENS, FILTERS), jnp.float32)
    for group in range(N_CHAN):
        first = group * FILTERS
        cot_in = grad_out[first:first + FILTERS, :].T.astype(jnp.float32)
        gate_q = query[first:first + FILTERS, :].T.astype(jnp.float32)
        gate_k = key_proj[first:first + FILTERS, :].T.astype(jnp.float32)
        gate_v = value[first:first + FILTERS, :].T.astype(jnp.float32)
        signal = gate_k * gate_v
        cot = cot_in * gate_q
        signal_spec = jnp.fft.rfft(signal, n=padded, axis=0)
        cot_spec = jnp.fft.rfft(cot, n=padded, axis=0)
        conv = jnp.fft.irfft(filter_spec * signal_spec, n=padded, axis=0)[:TOKENS]
        grad_signal = jnp.fft.irfft(jnp.conj(filter_spec) * cot_spec, n=padded, axis=0)[:TOKENS]
        filter_total = filter_total + jnp.fft.irfft(cot_spec * jnp.conj(signal_spec), n=padded, axis=0)[:TOKENS]
        dq_list.append((cot_in * conv).T.astype(jnp.bfloat16))
        dk_list.append((grad_signal * gate_v).T.astype(jnp.bfloat16))
        dv_list.append((grad_signal * gate_k).T.astype(jnp.bfloat16))
    grad_query = jnp.concatenate(dq_list, axis=0)
    grad_key = jnp.concatenate(dk_list, axis=0)
    grad_value = jnp.concatenate(dv_list, axis=0)
    grad_filter = (filter_total * filter_scale).T
    return (grad_query, grad_key, grad_value, grad_filter)
```

```python
import functools
import math

import jax
import jax.numpy as jnp
from jax import lax
from jax.experimental import pallas as pl
from jax.experimental.pallas import tpu as pltpu
from jax.sharding import PartitionSpec as P

LANES = 128
WIDE = 256
STEPS = 16
GROUP = 4
F32 = jnp.float32
BF16 = jnp.bfloat16


def position(merged):
    n_chan = lax.axis_size("chan") if merged else 1
    here = lax.axis_index("ctx") * n_chan
    return here + lax.axis_index("chan") if merged else here


def target(linear, n_merge):
    if n_merge == 1:
        return {"ctx": linear}
    return {"ctx": linear // n_merge, "chan": linear % n_merge}


def greet(me, peers, n_merge):
    barrier = pltpu.get_barrier_semaphore()

    def signal(step, carry):
        pl.semaphore_signal(
            barrier,
            inc=1,
            device_id=target((me + step) % peers, n_merge),
            device_id_type=pl.DeviceIdType.MESH,
        )
        return carry

    lax.fori_loop(1, peers, signal, 0)
    pl.semaphore_wait(barrier, peers - 1)


def chunk_copy(src, dst, send_sem, recv_sem, peer, n_merge):
    return pltpu.make_async_remote_copy(
        src_ref=src,
        dst_ref=dst,
        send_sem=send_sem,
        recv_sem=recv_sem,
        device_id=target(peer, n_merge),
        device_id_type=pl.DeviceIdType.MESH,
    )


def split_rows(values, stage, start, stride):
    rows, width = values.shape
    for k in range(width // LANES):
        stage[pl.ds(start + k, rows, stride=stride), :] = values[:, k * LANES : (k + 1) * LANES]


def gather_kernel(peers, n_merge, scale, go_ref, q_ref, k_ref, v_ref, f_ref, data_ref, filt_ref,
                  stage, fstage, send_sem, recv_sem, fsend_sem, frecv_sem):
    me = position(n_merge > 1)
    tiles = go_ref.shape[1] // LANES
    n_ctx = peers // n_merge
    split_rows(k_ref[...].astype(F32) * v_ref[...].astype(F32), stage, 0, 2 * tiles)
    split_rows(go_ref[...].astype(F32) * q_ref[...].astype(F32), stage, tiles, 2 * tiles)
    split_rows(f_ref[...] * scale, fstage, 0, tiles)
    greet(me, peers, n_merge)
    size = 2 * tiles

    def data_copy(src_row, dst_row, send, recv, peer):
        return chunk_copy(
            stage.at[pl.ds(pl.multiple_of(src_row * size, 8), size), :],
            data_ref.at[pl.ds(pl.multiple_of(dst_row * size, 8), size), :],
            send_sem.at[send], recv_sem.at[recv], peer, n_merge,
        )

    def filt_copy(src_row, dst_row, send, recv, peer):
        return chunk_copy(
            fstage.at[pl.ds(pl.multiple_of(src_row * tiles, 8), tiles), :],
            filt_ref.at[pl.ds(pl.multiple_of(dst_row * tiles, 8), tiles), :],
            fsend_sem.at[send], frecv_sem.at[recv], peer, n_merge,
        )

    my_ctx = me // n_merge

    def send_filt(step, carry):
        peer = (me + step * n_merge) % peers
        filt_copy(peer, my_ctx, peer // n_merge, my_ctx, peer).start()
        return carry

    def send_data(step, carry):
        peer = (me + step) % peers
        data_copy(peer, me, peer, me, peer).start()
        return carry

    lax.fori_loop(1, n_ctx, send_filt, 0)
    lax.fori_loop(1, peers, send_data, 0)
    data_ref[pl.ds(pl.multiple_of(me * size, 8), size), :] = stage[pl.ds(pl.multiple_of(me * size, 8), size), :]
    filt_ref[pl.ds(pl.multiple_of(my_ctx * tiles, 8), tiles), :] = fstage[
        pl.ds(pl.multiple_of(me * tiles, 8), tiles), :
    ]

    def wait_filt(step, carry):
        peer = (me + step * n_merge) % peers
        copy = filt_copy(peer, peer // n_merge, peer // n_merge, peer // n_merge, peer)
        copy.wait_recv()
        copy.wait_send()
        return carry

    def wait_data(step, carry):
        peer = (me + step) % peers
        copy = data_copy(peer, peer, peer, peer, peer)
        copy.wait_recv()
        copy.wait_send()
        return carry

    lax.fori_loop(1, n_ctx, wait_filt, 0)
    lax.fori_loop(1, peers, wait_data, 0)


def scatter_kernel(peers, n_merge, go_ref, k_ref, v_ref, part_ref, dq_ref, dk_ref, dv_ref, df_ref,
                   landed, send_sem, recv_sem):
    me = position(n_merge > 1)
    rows, width = go_ref.shape
    tiles = width // LANES
    size = 3 * tiles
    greet(me, peers, n_merge)

    def copy_of(src_row, dst_row, send, recv, peer):
        return chunk_copy(
            part_ref.at[pl.ds(pl.multiple_of(src_row * size, 8), size), :],
            landed.at[pl.ds(pl.multiple_of(dst_row * size, 8), size), :],
            send_sem.at[send], recv_sem.at[recv], peer, n_merge,
        )

    def send(step, carry):
        peer = (me + step) % peers
        copy_of(peer, me, peer, me, peer).start()
        return carry

    lax.fori_loop(1, peers, send, 0)
    landed[pl.ds(pl.multiple_of(me * size, 8), size), :] = part_ref[pl.ds(pl.multiple_of(me * size, 8), size), :]

    def wait(step, carry):
        peer = (me + step) % peers
        copy = copy_of(peer, peer, peer, peer, peer)
        copy.wait_recv()
        copy.wait_send()
        return carry

    lax.fori_loop(1, peers, wait, 0)
    for k in range(tiles):
        cols = slice(k * LANES, (k + 1) * LANES)
        conv = landed[pl.ds(k, rows, stride=size), :]
        back = landed[pl.ds(tiles + k, rows, stride=size), :]
        dq_ref[:, cols] = (go_ref[:, cols].astype(F32) * conv).astype(BF16)
        dk_ref[:, cols] = (back * v_ref[:, cols].astype(F32)).astype(BF16)
        dv_ref[:, cols] = (back * k_ref[:, cols].astype(F32)).astype(BF16)
        df_ref[:, cols] = landed[pl.ds(2 * tiles + k, rows, stride=size), :]


def convolve_kernel(n_ctx, n_merge, tiles, scale, data_ref, filt_ref, out_ref, flat, pad, toep, acc, gacc):
    blocks = n_ctx * tiles
    half = blocks // 2
    span = half + STEPS
    lane = lax.broadcasted_iota(jnp.int32, (LANES, LANES), 1)
    row = lax.broadcasted_iota(jnp.int32, (LANES, LANES), 0)
    flip = (lane + row == LANES - 1).astype(F32)
    keep = lane >= row

    def reverse(values):
        return jnp.dot(values, flip, precision=lax.Precision.HIGHEST, preferred_element_type=F32)

    for src in range(n_ctx):
        flat[src * tiles : (src + 1) * tiles, :] = filt_ref[src * tiles : (src + 1) * tiles, :]
        for ch in range(n_merge):
            for a in range(2):
                at = ((src * n_merge + ch) * 2 + a) * tiles
                to = (1 + 2 * ch + a) * blocks + src * tiles
                flat[to : to + tiles, :] = data_ref[at : at + tiles, :]
    zeros = jnp.zeros((STEPS, WIDE), F32)
    for ch in range(n_merge):
        first = (1 + 2 * ch) * blocks
        pad[2 * ch, 0:STEPS, :] = zeros
        pad[2 * ch, STEPS:span, 0:LANES] = flat[pl.ds(first, half, stride=2), :]
        pad[2 * ch, STEPS:span, LANES:WIDE] = flat[pl.ds(first + 1, half, stride=2), :]
        first = (2 + 2 * ch) * blocks
        pad[2 * ch + 1, half:span, :] = zeros
        pad[2 * ch + 1, 0:half, 0:LANES] = reverse(flat[pl.ds(first + 1, half, stride=2), :])
        pad[2 * ch + 1, 0:half, LANES:WIDE] = reverse(flat[pl.ds(first, half, stride=2), :])

    for n in range(1 + n_merge):
        first = 0 if n == 0 else (2 * n - 1) * blocks
        toep[n, LANES:WIDE, 0:LANES] = jnp.zeros((LANES, LANES), BF16)

        def skew(block, n=n, first=first):
            wide = jnp.broadcast_to(flat[pl.ds(first + block, 1), :], (LANES, LANES))
            return pltpu.roll(wide, 0, 1, stride=1, stride_axis=0)

        def build(d, before, n=n, skew=skew):
            even = skew(2 * d)
            odd = skew(2 * d + 1)
            at = pl.multiple_of(d * WIDE, WIDE)
            low = jnp.where(keep, even, before).astype(BF16)
            high = jnp.where(keep, odd, even).astype(BF16)
            toep[n, pl.ds(at, LANES), 0:LANES] = low
            toep[n, pl.ds(at, LANES), LANES:WIDE] = high
            toep[n, pl.ds(at + LANES, LANES), LANES:WIDE] = low
            toep[n, pl.ds(at + WIDE + LANES, LANES), 0:LANES] = high
            return odd

        lax.fori_loop(0, half, build, jnp.zeros((LANES, LANES), F32))

    acc[...] = jnp.zeros_like(acc)
    gacc[...] = jnp.zeros_like(gacc)
    for q in range(half // STEPS):
        n = half - q * STEPS

        for g in range(STEPS // GROUP):
            at = (q * STEPS + g * GROUP) * WIDE
            shifts = [g * GROUP + s for s in range(GROUP)]
            down = [
                jnp.concatenate([pad[2 * ch, pl.ds(STEPS - dd, n), :].astype(BF16) for dd in shifts], axis=1)
                for ch in range(n_merge)
            ]
            up = [
                jnp.concatenate(
                    [pad[2 * ch + 1, pl.ds(q * STEPS + dd, n), :].astype(BF16) for dd in shifts], axis=1
                )
                for ch in range(n_merge)
            ]
            both = jnp.concatenate(down + up, axis=0)
            prod = jnp.dot(both, toep[0, pl.ds(at, GROUP * WIDE), :], preferred_element_type=F32)
            total = None
            for ch in range(n_merge):
                acc[ch, q * STEPS : half, :] += prod[ch * n : (ch + 1) * n]
                acc[n_merge + ch, 0:n, :] += prod[(n_merge + ch) * n : (n_merge + ch + 1) * n]
                part = jnp.dot(up[ch], toep[1 + ch, pl.ds(at, GROUP * WIDE), :], preferred_element_type=F32)
                total = part if total is None else total + part
            gacc[0:n, :] += total

    for ch in range(n_merge):
        flat[pl.ds(2 * ch * blocks, half, stride=2), :] = acc[ch, :, 0:LANES]
        flat[pl.ds(2 * ch * blocks + 1, half, stride=2), :] = acc[ch, :, LANES:WIDE]
        flat[pl.ds((2 * ch + 1) * blocks, half, stride=2), :] = reverse(acc[n_merge + ch, :, LANES:WIDE])
        flat[pl.ds((2 * ch + 1) * blocks + 1, half, stride=2), :] = reverse(acc[n_merge + ch, :, 0:LANES])
    first = 2 * n_merge * blocks
    flat[pl.ds(first, half, stride=2), :] = reverse(gacc[:, LANES:WIDE]) * scale
    flat[pl.ds(first + 1, half, stride=2), :] = reverse(gacc[:, 0:LANES]) * scale
    for src in range(n_ctx):
        for ch in range(n_merge):
            for a in range(3):
                at = ((src * n_merge + ch) * 3 + a) * tiles
                of = (2 * ch + a if a < 2 else 2 * n_merge) * blocks + src * tiles
                out_ref[at : at + tiles, :] = flat[of : of + tiles, :]


def vmem(count):
    return [pl.BlockSpec(memory_space=pltpu.VMEM)] * count


def local(grad_out, query, key_proj, value, filter_param):
    n_ctx = lax.axis_size("ctx")
    n_chan = lax.axis_size("chan")
    rows, width = grad_out.shape
    tiles = width // LANES
    n_merge = n_chan if rows == n_ctx * n_chan else 1
    peers = n_ctx * n_merge
    if rows != peers or filter_param.shape[0] != rows:
        raise ValueError("unsupported sizes")
    scale = 1.0 / math.sqrt(n_ctx * width)
    blocks = n_ctx * tiles
    half = blocks // 2
    dma = pltpu.SemaphoreType.DMA
    data, filt = pl.pallas_call(
        functools.partial(gather_kernel, peers, n_merge, scale),
        out_shape=(
            jax.ShapeDtypeStruct((peers * 2 * tiles, LANES), F32),
            jax.ShapeDtypeStruct((blocks, LANES), F32),
        ),
        in_specs=vmem(5),
        out_specs=tuple(vmem(2)),
        scratch_shapes=[
            pltpu.VMEM((peers * 2 * tiles, LANES), F32),
            pltpu.VMEM((peers * tiles, LANES), F32),
            dma((peers,)),
            dma((peers,)),
            dma((n_ctx,)),
            dma((n_ctx,)),
        ],
        compiler_params=pltpu.CompilerParams(collective_id=0, has_side_effects=True),
        name="gather_channels",
    )(grad_out, query, key_proj, value, filter_param)
    parts = pl.pallas_call(
        functools.partial(convolve_kernel, n_ctx, n_merge, tiles, scale),
        out_shape=jax.ShapeDtypeStruct((peers * 3 * tiles, LANES), F32),
        in_specs=vmem(2),
        out_specs=vmem(1)[0],
        scratch_shapes=[
            pltpu.VMEM(((2 * n_merge + 1) * blocks, LANES), F32),
            pltpu.VMEM((2 * n_merge, half + STEPS, WIDE), F32),
            pltpu.VMEM((1 + n_merge, (half + 1) * WIDE, WIDE), BF16),
            pltpu.VMEM((2 * n_merge, half, WIDE), F32),
            pltpu.VMEM((half, WIDE), F32),
        ],
        compiler_params=pltpu.CompilerParams(vmem_limit_bytes=56 * 1024 * 1024),
        name="long_convolutions",
    )(data, filt)
    dq, dk, dv, df = pl.pallas_call(
        functools.partial(scatter_kernel, peers, n_merge),
        out_shape=(
            jax.ShapeDtypeStruct((rows, width), BF16),
            jax.ShapeDtypeStruct((rows, width), BF16),
            jax.ShapeDtypeStruct((rows, width), BF16),
            jax.ShapeDtypeStruct((rows, width), F32),
        ),
        in_specs=vmem(4),
        out_specs=tuple(vmem(4)),
        scratch_shapes=[
            pltpu.VMEM((peers * 3 * tiles, LANES), F32),
            dma((peers,)),
            dma((peers,)),
        ],
        compiler_params=pltpu.CompilerParams(collective_id=1, has_side_effects=True),
        name="scatter_positions",
    )(grad_out, key_proj, value, parts)
    if n_merge == 1:
        df = lax.psum(df, "chan")
    return (dq, dk, dv, df)


def solution(mesh):
    in_specs = (
        P("chan", "ctx"),
        P("chan", "ctx"),
        P("chan", "ctx"),
        P("chan", "ctx"),
        P(None, "ctx"),
    )
    out_specs = (P("chan", "ctx"), P("chan", "ctx"), P("chan", "ctx"), P(None, "ctx"))
    return jax.shard_map(local, mesh=mesh, in_specs=in_specs, out_specs=out_specs, check_vma=False)
```

```python
import functools
import math

import jax
import jax.numpy as jnp
from jax import lax
from jax.experimental import pallas as pl
from jax.experimental.pallas import tpu as pltpu
from jax.sharding import PartitionSpec as P

LANES = 128
STEPS = 16
DEPTH = STEPS * LANES
F32 = jnp.float32
BF16 = jnp.bfloat16


def rows_at(ref, start, count):
    return ref.at[pl.ds(pl.multiple_of(start, 8), count), :]


def split_rows(values, stage, tiles):
    for k in range(tiles):
        stage[pl.ds(k, values.shape[0], stride=tiles), :] = values[:, k * LANES : (k + 1) * LANES]


def convolve_kernel(n_ctx, n_merge, scale, go_ref, q_ref, k_ref, v_ref, f_ref, landed_ref,
                    f_stage, s_stage, c_stage, f_land, s_land, c_land, c_pad, s_lhs, c_lhs, toep,
                    conv, back, corr, send_sem, recv_sem, own_sem):
    tiles = go_ref.shape[1] // LANES
    blocks = n_ctx * tiles
    span = blocks + STEPS
    peers = n_ctx * n_merge
    my_ctx = lax.axis_index("ctx")
    my_chan = lax.axis_index("chan") if n_merge > 1 else 0
    me = my_ctx * n_merge + my_chan

    offsets = [(c, j) for c in range(n_ctx) for j in range(n_merge) if (c, j) != (0, 0)]
    offsets.sort(key=lambda o: (abs(o[0] - n_ctx // 2), o))
    others = []
    for c, j in offsets:
        ctx = (my_ctx + c) % n_ctx
        chan = (my_chan + j) % n_merge if n_merge > 1 else 0
        ident = {"ctx": ctx, "chan": chan} if n_merge > 1 else {"ctx": ctx}
        others.append((j == 0, ctx, chan, ctx * n_merge + chan, ident))

    barrier = pltpu.get_barrier_semaphore()
    for _, _, _, _, ident in others:
        pl.semaphore_signal(barrier, inc=1, device_id=ident, device_id_type=pl.DeviceIdType.MESH)

    def remote(src, dst, n, ident):
        return pltpu.make_async_remote_copy(
            src_ref=src, dst_ref=dst, send_sem=send_sem.at[n], recv_sem=recv_sem.at[n],
            device_id=ident, device_id_type=pl.DeviceIdType.MESH,
        )

    def whole(stage, n, count):
        part = stage.at[pl.ds(0, count * tiles), :]
        return remote(part, part, n, others[0][4])

    split_rows(f_ref[...] * scale, f_stage, tiles)
    split_rows(k_ref[...].astype(F32) * v_ref[...].astype(F32), s_stage, tiles)
    pl.semaphore_wait(barrier, peers - 1)
    for same, ctx, chan, peer, ident in others:
        if same:
            remote(rows_at(f_stage, peer * tiles, tiles), rows_at(f_land, my_ctx * tiles, tiles), 0, ident).start()
    for _, ctx, chan, peer, ident in others:
        remote(
            rows_at(s_stage, peer * tiles, tiles),
            rows_at(s_land, my_chan * span + STEPS + my_ctx * tiles, tiles), 1, ident,
        ).start()
    split_rows(go_ref[...].astype(F32) * q_ref[...].astype(F32), c_stage, tiles)
    for _, ctx, chan, peer, ident in others:
        remote(
            rows_at(c_stage, peer * tiles, tiles),
            rows_at(c_land, my_chan * blocks + my_ctx * tiles, tiles), 2, ident,
        ).start()
    mine = pl.ds(pl.multiple_of(me * tiles, 8), tiles)
    f_land[pl.ds(pl.multiple_of(my_ctx * tiles, 8), tiles), :] = f_stage[mine, :]
    s_land[pl.ds(pl.multiple_of(my_chan * span + STEPS + my_ctx * tiles, 8), tiles), :] = s_stage[mine, :]
    c_land[pl.ds(pl.multiple_of(my_chan * blocks + my_ctx * tiles, 8), tiles), :] = c_stage[mine, :]
    for ch in range(n_merge):
        s_land[ch * span : ch * span + STEPS, :] = jnp.zeros((STEPS, LANES), F32)
        c_pad[ch * span + blocks : (ch + 1) * span, :] = jnp.zeros((STEPS, LANES), F32)

    lane = lax.broadcasted_iota(jnp.int32, (LANES, LANES), 1)
    row = lax.broadcasted_iota(jnp.int32, (LANES, LANES), 0)
    flip = (lane + row == LANES - 1).astype(F32)
    current = lane < LANES - row

    def reverse(values):
        return jnp.dot(values, flip, precision=lax.Precision.HIGHEST, preferred_element_type=F32)

    def skew(before, now):
        picked = jnp.where(
            current, jnp.broadcast_to(now, (LANES, LANES)), jnp.broadcast_to(before, (LANES, LANES))
        )
        return pltpu.roll(picked, 0, 1, stride=1, stride_axis=0).astype(BF16)

    whole(f_stage, 0, n_ctx - 1).wait_recv()

    def build(src, before):
        rows = f_land[pl.ds(pl.multiple_of(src * tiles, 8), tiles), :]
        for k in range(tiles):
            now = rows[k : k + 1, :]
            toep[0, pl.ds(pl.multiple_of((src * tiles + k) * LANES, LANES), LANES), :] = skew(before, now)
            before = now
        return before

    lax.fori_loop(0, n_ctx, build, jnp.zeros((1, LANES), F32))
    whole(s_stage, 1, peers - 1).wait_recv()
    for ch in range(n_merge):
        for dd in range(STEPS):
            at = ch * span + STEPS - dd
            s_lhs[ch, :, dd * LANES : (dd + 1) * LANES] = s_land[at : at + blocks, :].astype(BF16)

    def band(n, g):
        return toep[n, g * DEPTH : (g + 1) * DEPTH, :]

    for g in range(blocks // STEPS):
        n = blocks - g * STEPS
        lhs = jnp.concatenate([s_lhs[ch, 0:n, :] for ch in range(n_merge)], axis=0)
        prod = jnp.dot(lhs, band(0, g), preferred_element_type=F32)
        for ch in range(n_merge):
            part = prod[ch * n : (ch + 1) * n]
            rows = slice(ch * blocks + g * STEPS, (ch + 1) * blocks)
            conv[rows, :] = part if g == 0 else conv[rows, :] + part
            for block in range(g * STEPS, (g + 1) * STEPS):
                at = ch * span + STEPS + block
                toep[1 + ch, block * LANES : (block + 1) * LANES, :] = skew(
                    s_land[at - 1 : at, :], s_land[at : at + 1, :]
                )

    def send_result(src_of, a):
        for _, ctx, chan, peer, ident in others:
            remote(src_of(ctx, chan), rows_at(landed_ref, (me * 3 + a) * tiles, tiles), 3 + a, ident).start()
        own = pltpu.make_async_copy(
            src_of(my_ctx, my_chan), rows_at(landed_ref, (me * 3 + a) * tiles, tiles), own_sem.at[a]
        )
        own.start()
        return own

    owns = [send_result(lambda ctx, chan: rows_at(conv, chan * blocks + ctx * tiles, tiles), 0)]

    whole(c_stage, 2, peers - 1).wait_recv()
    for ch in range(n_merge):
        c_pad[ch * span : ch * span + blocks, :] = reverse(c_land[ch * blocks : (ch + 1) * blocks, :])
        for dd in range(STEPS):
            at = ch * span + dd
            c_lhs[ch, :, dd * LANES : (dd + 1) * LANES] = c_pad[at : at + blocks, :].astype(BF16)

    for g in range(blocks // STEPS):
        n = blocks - g * STEPS
        lhs = jnp.concatenate([c_lhs[ch, g * STEPS : blocks, :] for ch in range(n_merge)], axis=0)
        prod = jnp.dot(lhs, band(0, g), preferred_element_type=F32)
        for ch in range(n_merge):
            part = prod[ch * n : (ch + 1) * n]
            rows = slice(ch * blocks, ch * blocks + n)
            back[rows, :] = part if g == 0 else back[rows, :] + part
    back[...] = reverse(back[...])
    owns.append(send_result(lambda ctx, chan: rows_at(back, chan * blocks + ctx * tiles, tiles), 1))

    for g in range(blocks // STEPS):
        n = blocks - g * STEPS
        for ch in range(n_merge):
            part = jnp.dot(c_lhs[ch, g * STEPS : blocks, :], band(1 + ch, g), preferred_element_type=F32)
            corr[0:n, :] = part if g == 0 and ch == 0 else corr[0:n, :] + part
    corr[...] = reverse(corr[...]) * scale
    owns.append(send_result(lambda ctx, chan: rows_at(corr, ctx * tiles, tiles), 2))

    whole(f_stage, 0, n_ctx - 1).wait_send()
    whole(s_stage, 1, peers - 1).wait_send()
    whole(c_stage, 2, peers - 1).wait_send()
    for a in range(3):
        owns[a].wait()
        whole(s_stage, 3 + a, peers - 1).wait_send()
        whole(s_stage, 3 + a, peers - 1).wait_recv()


def gate_kernel(go_ref, k_ref, v_ref, landed_ref, dq_ref, dk_ref, dv_ref, df_ref):
    rows, width = go_ref.shape
    tiles = width // LANES
    size = 3 * tiles
    for k in range(tiles):
        cols = slice(k * LANES, (k + 1) * LANES)
        conv = landed_ref[pl.ds(k, rows, stride=size), :]
        back = landed_ref[pl.ds(tiles + k, rows, stride=size), :]
        dq_ref[:, cols] = (go_ref[:, cols].astype(F32) * conv).astype(BF16)
        dk_ref[:, cols] = (back * v_ref[:, cols].astype(F32)).astype(BF16)
        dv_ref[:, cols] = (back * k_ref[:, cols].astype(F32)).astype(BF16)
        df_ref[:, cols] = landed_ref[pl.ds(2 * tiles + k, rows, stride=size), :]


def vmem(count):
    return [pl.BlockSpec(memory_space=pltpu.VMEM)] * count


def local(grad_out, query, key_proj, value, filter_param):
    n_ctx = lax.axis_size("ctx")
    n_chan = lax.axis_size("chan")
    rows, width = grad_out.shape
    tiles = width // LANES
    n_merge = n_chan if rows == n_ctx * n_chan else 1
    peers = n_ctx * n_merge
    blocks = n_ctx * tiles
    if rows != peers or filter_param.shape[0] != rows or tiles % 8 or blocks % STEPS:
        raise ValueError("unsupported sizes")
    scale = 1.0 / math.sqrt(n_ctx * width)
    span = blocks + STEPS
    dma = pltpu.SemaphoreType.DMA

    def buffer(*shape, dtype=F32):
        return pltpu.VMEM(shape, dtype)

    landed = pl.pallas_call(
        functools.partial(convolve_kernel, n_ctx, n_merge, scale),
        out_shape=jax.ShapeDtypeStruct((peers * 3 * tiles, LANES), F32),
        in_specs=vmem(5),
        out_specs=pl.BlockSpec(memory_space=pl.ANY),
        scratch_shapes=[
            buffer(rows * tiles, LANES),
            buffer(rows * tiles, LANES),
            buffer(rows * tiles, LANES),
            buffer(blocks, LANES),
            buffer(n_merge * span, LANES),
            buffer(n_merge * blocks, LANES),
            buffer(n_merge * span, LANES),
            buffer(n_merge, blocks, DEPTH, dtype=BF16),
            buffer(n_merge, blocks, DEPTH, dtype=BF16),
            buffer(1 + n_merge, blocks * LANES, LANES, dtype=BF16),
            buffer(n_merge * blocks, LANES),
            buffer(n_merge * blocks, LANES),
            buffer(blocks, LANES),
            dma((6,)),
            dma((6,)),
            dma((3,)),
        ],
        compiler_params=pltpu.CompilerParams(
            collective_id=0, has_side_effects=True, vmem_limit_bytes=48 * 1024 * 1024
        ),
        name="long_convolutions",
    )(grad_out, query, key_proj, value, filter_param)
    dq, dk, dv, df = pl.pallas_call(
        gate_kernel,
        out_shape=(
            jax.ShapeDtypeStruct((rows, width), BF16),
            jax.ShapeDtypeStruct((rows, width), BF16),
            jax.ShapeDtypeStruct((rows, width), BF16),
            jax.ShapeDtypeStruct((rows, width), F32),
        ),
        in_specs=vmem(4),
        out_specs=tuple(vmem(4)),
        name="gate_gradients",
    )(grad_out, key_proj, value, landed)
    if n_merge == 1:
        df = lax.psum(df, "chan")
    return (dq, dk, dv, df)


def solution(mesh):
    in_specs = (
        P("chan", "ctx"),
        P("chan", "ctx"),
        P("chan", "ctx"),
        P("chan", "ctx"),
        P(None, "ctx"),
    )
    out_specs = (P("chan", "ctx"), P("chan", "ctx"), P("chan", "ctx"), P(None, "ctx"))
    return jax.shard_map(local, mesh=mesh, in_specs=in_specs, out_specs=out_specs, check_vma=False)
```

```python
import functools
import math

import jax
import jax.numpy as jnp
from jax import lax
from jax.experimental import pallas as pl
from jax.experimental.pallas import tpu as pltpu
from jax.sharding import PartitionSpec as P

LANES = 128
STEPS = 16
VMEM_BYTES = 60 * 1024 * 1024
DEPTH = STEPS * LANES
F32 = jnp.float32
BF16 = jnp.bfloat16


def rows_at(ref, start, count):
    return ref.at[pl.ds(pl.multiple_of(start, 8), count), :]


def split_rows(values, stage, tiles):
    for k in range(tiles):
        stage[pl.ds(k, values.shape[0], stride=tiles), :] = values[:, k * LANES : (k + 1) * LANES]


def convolve_kernel(n_ctx, n_merge, scale, go_hbm, q_hbm, k_hbm, v_hbm, f_hbm, landed_ref,
                    go_ref, q_ref, k_ref, v_ref, f_ref, load_sem, f_stage, s_stage, c_stage, f_land, s_land, c_land, c_pad, s_lhs, c_lhs, toep,
                    conv, back, corr, send_sem, recv_sem, own_sem):
    loads = [
        pltpu.make_async_copy(src, dst, load_sem.at[n])
        for n, (src, dst) in enumerate(
            [(f_hbm, f_ref), (k_hbm, k_ref), (v_hbm, v_ref), (go_hbm, go_ref), (q_hbm, q_ref)]
        )
    ]
    for load in loads:
        load.start()
    tiles = go_ref.shape[1] // LANES
    blocks = n_ctx * tiles
    span = blocks + STEPS
    peers = n_ctx * n_merge
    my_ctx = lax.axis_index("ctx")
    my_chan = lax.axis_index("chan") if n_merge > 1 else 0
    me = my_ctx * n_merge + my_chan

    offsets = [(c, j) for c in range(n_ctx) for j in range(n_merge) if (c, j) != (0, 0)]
    offsets.sort(key=lambda o: (abs(o[0] - n_ctx // 2), o))
    others = []
    for c, j in offsets:
        ctx = (my_ctx + c) % n_ctx
        chan = (my_chan + j) % n_merge if n_merge > 1 else 0
        ident = {"ctx": ctx, "chan": chan} if n_merge > 1 else {"ctx": ctx}
        others.append((j == 0, ctx, chan, ctx * n_merge + chan, ident))

    barrier = pltpu.get_barrier_semaphore()
    for _, _, _, _, ident in others:
        pl.semaphore_signal(barrier, inc=1, device_id=ident, device_id_type=pl.DeviceIdType.MESH)

    def remote(src, dst, n, ident):
        return pltpu.make_async_remote_copy(
            src_ref=src, dst_ref=dst, send_sem=send_sem.at[n], recv_sem=recv_sem.at[n],
            device_id=ident, device_id_type=pl.DeviceIdType.MESH,
        )

    def whole(stage, n, count):
        part = stage.at[pl.ds(0, count * tiles), :]
        return remote(part, part, n, others[0][4])

    loads[0].wait()
    split_rows(f_ref[...] * scale, f_stage, tiles)
    loads[1].wait()
    loads[2].wait()
    split_rows(k_ref[...].astype(F32) * v_ref[...].astype(F32), s_stage, tiles)
    pl.semaphore_wait(barrier, peers - 1)
    for same, ctx, chan, peer, ident in others:
        if same:
            remote(rows_at(f_stage, peer * tiles, tiles), rows_at(f_land, my_ctx * tiles, tiles), 0, ident).start()
    for _, ctx, chan, peer, ident in others:
        remote(
            rows_at(s_stage, peer * tiles, tiles),
            rows_at(s_land, my_chan * span + STEPS + my_ctx * tiles, tiles), 1, ident,
        ).start()
    loads[3].wait()
    loads[4].wait()
    split_rows(go_ref[...].astype(F32) * q_ref[...].astype(F32), c_stage, tiles)
    for _, ctx, chan, peer, ident in others:
        remote(
            rows_at(c_stage, peer * tiles, tiles),
            rows_at(c_land, my_chan * blocks + my_ctx * tiles, tiles), 2, ident,
        ).start()
    mine = pl.ds(pl.multiple_of(me * tiles, 8), tiles)
    f_land[pl.ds(pl.multiple_of(my_ctx * tiles, 8), tiles), :] = f_stage[mine, :]
    s_land[pl.ds(pl.multiple_of(my_chan * span + STEPS + my_ctx * tiles, 8), tiles), :] = s_stage[mine, :]
    c_land[pl.ds(pl.multiple_of(my_chan * blocks + my_ctx * tiles, 8), tiles), :] = c_stage[mine, :]
    for ch in range(n_merge):
        s_land[ch * span : ch * span + STEPS, :] = jnp.zeros((STEPS, LANES), F32)
        c_pad[ch * span + blocks : (ch + 1) * span, :] = jnp.zeros((STEPS, LANES), F32)

    lane = lax.broadcasted_iota(jnp.int32, (LANES, LANES), 1)
    row = lax.broadcasted_iota(jnp.int32, (LANES, LANES), 0)
    flip = (lane + row == LANES - 1).astype(F32)
    current = lane < LANES - row

    def reverse(values):
        return jnp.dot(values, flip, precision=lax.Precision.HIGHEST, preferred_element_type=F32)

    def skew(before, now):
        picked = jnp.where(
            current, jnp.broadcast_to(now, (LANES, LANES)), jnp.broadcast_to(before, (LANES, LANES))
        )
        return pltpu.roll(picked, 0, 1, stride=1, stride_axis=0).astype(BF16)

    whole(f_stage, 0, n_ctx - 1).wait_recv()

    def build(src, before):
        rows = f_land[pl.ds(pl.multiple_of(src * tiles, 8), tiles), :]
        for k in range(tiles):
            now = rows[k : k + 1, :]
            toep[0, pl.ds(pl.multiple_of((src * tiles + k) * LANES, LANES), LANES), :] = skew(before, now)
            before = now
        return before

    lax.fori_loop(0, n_ctx, build, jnp.zeros((1, LANES), F32))
    whole(s_stage, 1, peers - 1).wait_recv()
    for ch in range(n_merge):
        for dd in range(STEPS):
            at = ch * span + STEPS - dd
            s_lhs[ch, :, dd * LANES : (dd + 1) * LANES] = s_land[at : at + blocks, :].astype(BF16)

    def band(n, g):
        return toep[n, g * DEPTH : (g + 1) * DEPTH, :]

    for g in range(blocks // STEPS):
        n = blocks - g * STEPS
        lhs = jnp.concatenate([s_lhs[ch, 0:n, :] for ch in range(n_merge)], axis=0)
        prod = jnp.dot(lhs, band(0, g), preferred_element_type=F32)
        for ch in range(n_merge):
            part = prod[ch * n : (ch + 1) * n]
            rows = slice(ch * blocks + g * STEPS, (ch + 1) * blocks)
            conv[rows, :] = part if g == 0 else conv[rows, :] + part
            for block in range(g * STEPS, (g + 1) * STEPS):
                at = ch * span + STEPS + block
                toep[1 + ch, block * LANES : (block + 1) * LANES, :] = skew(
                    s_land[at - 1 : at, :], s_land[at : at + 1, :]
                )

    def send_result(src_of, a):
        for _, ctx, chan, peer, ident in others:
            remote(src_of(ctx, chan), rows_at(landed_ref, (me * 3 + a) * tiles, tiles), 3 + a, ident).start()
        own = pltpu.make_async_copy(
            src_of(my_ctx, my_chan), rows_at(landed_ref, (me * 3 + a) * tiles, tiles), own_sem.at[a]
        )
        own.start()
        return own

    owns = [send_result(lambda ctx, chan: rows_at(conv, chan * blocks + ctx * tiles, tiles), 0)]

    whole(c_stage, 2, peers - 1).wait_recv()
    for ch in range(n_merge):
        c_pad[ch * span : ch * span + blocks, :] = reverse(c_land[ch * blocks : (ch + 1) * blocks, :])
        for dd in range(STEPS):
            at = ch * span + dd
            c_lhs[ch, :, dd * LANES : (dd + 1) * LANES] = c_pad[at : at + blocks, :].astype(BF16)

    for g in range(blocks // STEPS):
        n = blocks - g * STEPS
        lhs = jnp.concatenate([c_lhs[ch, g * STEPS : blocks, :] for ch in range(n_merge)], axis=0)
        prod = jnp.dot(lhs, band(0, g), preferred_element_type=F32)
        for ch in range(n_merge):
            part = prod[ch * n : (ch + 1) * n]
            rows = slice(ch * blocks, ch * blocks + n)
            back[rows, :] = part if g == 0 else back[rows, :] + part
    back[...] = reverse(back[...])
    owns.append(send_result(lambda ctx, chan: rows_at(back, chan * blocks + ctx * tiles, tiles), 1))

    for g in range(blocks // STEPS):
        n = blocks - g * STEPS
        for ch in range(n_merge):
            part = jnp.dot(c_lhs[ch, g * STEPS : blocks, :], band(1 + ch, g), preferred_element_type=F32)
            corr[0:n, :] = part if g == 0 and ch == 0 else corr[0:n, :] + part
    corr[...] = reverse(corr[...]) * scale
    owns.append(send_result(lambda ctx, chan: rows_at(corr, ctx * tiles, tiles), 2))

    whole(f_stage, 0, n_ctx - 1).wait_send()
    whole(s_stage, 1, peers - 1).wait_send()
    whole(c_stage, 2, peers - 1).wait_send()
    for a in range(3):
        owns[a].wait()
        whole(s_stage, 3 + a, peers - 1).wait_send()
        whole(s_stage, 3 + a, peers - 1).wait_recv()


def gate_kernel(go_ref, k_ref, v_ref, landed_ref, dq_ref, dk_ref, dv_ref, df_ref):
    rows, width = go_ref.shape
    tiles = width // LANES
    size = 3 * tiles
    for k in range(tiles):
        cols = slice(k * LANES, (k + 1) * LANES)
        conv = landed_ref[pl.ds(k, rows, stride=size), :]
        back = landed_ref[pl.ds(tiles + k, rows, stride=size), :]
        dq_ref[:, cols] = (go_ref[:, cols].astype(F32) * conv).astype(BF16)
        dk_ref[:, cols] = (back * v_ref[:, cols].astype(F32)).astype(BF16)
        dv_ref[:, cols] = (back * k_ref[:, cols].astype(F32)).astype(BF16)
        df_ref[:, cols] = landed_ref[pl.ds(2 * tiles + k, rows, stride=size), :]


def vmem(count):
    return [pl.BlockSpec(memory_space=pltpu.VMEM)] * count


def local(grad_out, query, key_proj, value, filter_param):
    n_ctx = lax.axis_size("ctx")
    n_chan = lax.axis_size("chan")
    rows, width = grad_out.shape
    tiles = width // LANES
    n_merge = n_chan if rows == n_ctx * n_chan else 1
    peers = n_ctx * n_merge
    blocks = n_ctx * tiles
    if rows != peers or filter_param.shape[0] != rows or tiles % 8 or blocks % STEPS:
        raise ValueError("unsupported sizes")
    scale = 1.0 / math.sqrt(n_ctx * width)
    span = blocks + STEPS
    dma = pltpu.SemaphoreType.DMA

    def buffer(*shape, dtype=F32):
        return pltpu.VMEM(shape, dtype)

    landed = pl.pallas_call(
        functools.partial(convolve_kernel, n_ctx, n_merge, scale),
        out_shape=jax.ShapeDtypeStruct((peers * 3 * tiles, LANES), F32),
        in_specs=[pl.BlockSpec(memory_space=pl.ANY)] * 5,
        out_specs=pl.BlockSpec(memory_space=pl.ANY),
        scratch_shapes=[
            buffer(rows, width, dtype=BF16),
            buffer(rows, width, dtype=BF16),
            buffer(rows, width, dtype=BF16),
            buffer(rows, width, dtype=BF16),
            buffer(rows, width),
            dma((5,)),
            buffer(rows * tiles, LANES),
            buffer(rows * tiles, LANES),
            buffer(rows * tiles, LANES),
            buffer(blocks, LANES),
            buffer(n_merge * span, LANES),
            buffer(n_merge * blocks, LANES),
            buffer(n_merge * span, LANES),
            buffer(n_merge, blocks, DEPTH, dtype=BF16),
            buffer(n_merge, blocks, DEPTH, dtype=BF16),
            buffer(1 + n_merge, blocks * LANES, LANES, dtype=BF16),
            buffer(n_merge * blocks, LANES),
            buffer(n_merge * blocks, LANES),
            buffer(blocks, LANES),
            dma((6,)),
            dma((6,)),
            dma((3,)),
        ],
        compiler_params=pltpu.CompilerParams(
            collective_id=0, has_side_effects=True, vmem_limit_bytes=VMEM_BYTES
        ),
        name="long_convolutions",
    )(grad_out, query, key_proj, value, filter_param)
    dq, dk, dv, df = pl.pallas_call(
        gate_kernel,
        out_shape=(
            jax.ShapeDtypeStruct((rows, width), BF16),
            jax.ShapeDtypeStruct((rows, width), BF16),
            jax.ShapeDtypeStruct((rows, width), BF16),
            jax.ShapeDtypeStruct((rows, width), F32),
        ),
        in_specs=vmem(4),
        out_specs=tuple(vmem(4)),
        compiler_params=pltpu.CompilerParams(vmem_limit_bytes=VMEM_BYTES),
        name="gate_gradients",
    )(grad_out, key_proj, value, landed)
    if n_merge == 1:
        df = lax.psum(df, "chan")
    return (dq, dk, dv, df)


def solution(mesh):
    in_specs = (
        P("chan", "ctx"),
        P("chan", "ctx"),
        P("chan", "ctx"),
        P("chan", "ctx"),
        P(None, "ctx"),
    )
    out_specs = (P("chan", "ctx"), P("chan", "ctx"), P("chan", "ctx"), P(None, "ctx"))
    return jax.shard_map(local, mesh=mesh, in_specs=in_specs, out_specs=out_specs, check_vma=False)
```

```python
import functools
import math

import jax
import jax.numpy as jnp
from jax import lax
from jax.experimental import pallas as pl
from jax.experimental.pallas import tpu as pltpu
from jax.sharding import PartitionSpec as P

LANES = 128
STEPS = 16
VMEM_BYTES = 60 * 1024 * 1024
DEPTH = STEPS * LANES
F32 = jnp.float32
BF16 = jnp.bfloat16


def rows_at(ref, start, count):
    return ref.at[pl.ds(pl.multiple_of(start, 8), count), :]


def split_rows(values, stage, tiles):
    for k in range(tiles):
        stage[pl.ds(k, values.shape[0], stride=tiles), :] = values[:, k * LANES : (k + 1) * LANES]


def convolve_kernel(n_ctx, n_merge, scale, go_hbm, q_hbm, k_hbm, v_hbm, f_hbm, landed_ref,
                    go_ref, q_ref, k_ref, v_ref, f_ref, load_sem, f_stage, s_stage, c_stage, f_land, s_land, c_land, c_pad, s_lhs, c_lhs, toep,
                    conv, back, corr, send_sem, recv_sem, own_sem):
    loads = [
        pltpu.make_async_copy(src, dst, load_sem.at[n])
        for n, (src, dst) in enumerate(
            [(f_hbm, f_ref), (k_hbm, k_ref), (v_hbm, v_ref), (go_hbm, go_ref), (q_hbm, q_ref)]
        )
    ]
    for load in loads:
        load.start()
    tiles = go_ref.shape[1] // LANES
    blocks = n_ctx * tiles
    span = blocks + STEPS
    peers = n_ctx * n_merge
    my_ctx = lax.axis_index("ctx")
    my_chan = lax.axis_index("chan") if n_merge > 1 else 0
    me = my_chan * n_ctx + my_ctx

    offsets = [(c, j) for c in range(n_ctx) for j in range(n_merge) if (c, j) != (0, 0)]
    offsets.sort(key=lambda o: (abs(o[0] - n_ctx // 2), o))
    others = []
    for c, j in offsets:
        ctx = (my_ctx + c) % n_ctx
        chan = (my_chan + j) % n_merge if n_merge > 1 else 0
        ident = {"ctx": ctx, "chan": chan} if n_merge > 1 else {"ctx": ctx}
        others.append((j == 0, ctx, chan, chan * n_ctx + ctx, ident))

    barrier = pltpu.get_barrier_semaphore()
    for _, _, _, _, ident in others:
        pl.semaphore_signal(barrier, inc=1, device_id=ident, device_id_type=pl.DeviceIdType.MESH)

    def remote(src, dst, n, ident):
        return pltpu.make_async_remote_copy(
            src_ref=src, dst_ref=dst, send_sem=send_sem.at[n], recv_sem=recv_sem.at[n],
            device_id=ident, device_id_type=pl.DeviceIdType.MESH,
        )

    def whole(stage, n, count):
        part = stage.at[pl.ds(0, count * tiles), :]
        return remote(part, part, n, others[0][4])

    loads[0].wait()
    split_rows(f_ref[...] * scale, f_stage, tiles)
    loads[1].wait()
    loads[2].wait()
    split_rows(k_ref[...].astype(F32) * v_ref[...].astype(F32), s_stage, tiles)
    pl.semaphore_wait(barrier, peers - 1)
    for same, ctx, chan, peer, ident in others:
        if same:
            remote(rows_at(f_stage, peer * tiles, tiles), rows_at(f_land, my_ctx * tiles, tiles), 0, ident).start()
    for _, ctx, chan, peer, ident in others:
        remote(
            rows_at(s_stage, peer * tiles, tiles),
            rows_at(s_land, my_chan * span + STEPS + my_ctx * tiles, tiles), 1, ident,
        ).start()
    loads[3].wait()
    loads[4].wait()
    split_rows(go_ref[...].astype(F32) * q_ref[...].astype(F32), c_stage, tiles)
    for _, ctx, chan, peer, ident in others:
        remote(
            rows_at(c_stage, peer * tiles, tiles),
            rows_at(c_land, my_chan * blocks + my_ctx * tiles, tiles), 2, ident,
        ).start()
    mine = pl.ds(pl.multiple_of(me * tiles, 8), tiles)
    f_land[pl.ds(pl.multiple_of(my_ctx * tiles, 8), tiles), :] = f_stage[mine, :]
    s_land[pl.ds(pl.multiple_of(my_chan * span + STEPS + my_ctx * tiles, 8), tiles), :] = s_stage[mine, :]
    c_land[pl.ds(pl.multiple_of(my_chan * blocks + my_ctx * tiles, 8), tiles), :] = c_stage[mine, :]
    for ch in range(n_merge):
        s_land[ch * span : ch * span + STEPS, :] = jnp.zeros((STEPS, LANES), F32)
        c_pad[ch * span + blocks : (ch + 1) * span, :] = jnp.zeros((STEPS, LANES), F32)

    lane = lax.broadcasted_iota(jnp.int32, (LANES, LANES), 1)
    row = lax.broadcasted_iota(jnp.int32, (LANES, LANES), 0)
    flip = (lane + row == LANES - 1).astype(F32)
    current = lane < LANES - row

    def reverse(values):
        return jnp.dot(values, flip, precision=lax.Precision.HIGHEST, preferred_element_type=F32)

    def skew(before, now):
        picked = jnp.where(
            current, jnp.broadcast_to(now, (LANES, LANES)), jnp.broadcast_to(before, (LANES, LANES))
        )
        return pltpu.roll(picked, 0, 1, stride=1, stride_axis=0).astype(BF16)

    whole(f_stage, 0, n_ctx - 1).wait_recv()

    def build(src, before):
        rows = f_land[pl.ds(pl.multiple_of(src * tiles, 8), tiles), :]
        for k in range(tiles):
            now = rows[k : k + 1, :]
            toep[0, pl.ds(pl.multiple_of((src * tiles + k) * LANES, LANES), LANES), :] = skew(before, now)
            before = now
        return before

    lax.fori_loop(0, n_ctx, build, jnp.zeros((1, LANES), F32))
    whole(s_stage, 1, peers - 1).wait_recv()
    for ch in range(n_merge):
        for dd in range(STEPS):
            at = ch * span + STEPS - dd
            s_lhs[ch, :, dd * LANES : (dd + 1) * LANES] = s_land[at : at + blocks, :].astype(BF16)

    def band(n, g):
        return toep[n, g * DEPTH : (g + 1) * DEPTH, :]

    for g in range(blocks // STEPS):
        n = blocks - g * STEPS
        lhs = jnp.concatenate([s_lhs[ch, 0:n, :] for ch in range(n_merge)], axis=0)
        prod = jnp.dot(lhs, band(0, g), preferred_element_type=F32)
        for ch in range(n_merge):
            part = prod[ch * n : (ch + 1) * n]
            rows = slice(ch * blocks + g * STEPS, (ch + 1) * blocks)
            conv[rows, :] = part if g == 0 else conv[rows, :] + part
            for block in range(g * STEPS, (g + 1) * STEPS):
                at = ch * span + STEPS + block
                toep[1 + ch, block * LANES : (block + 1) * LANES, :] = skew(
                    s_land[at - 1 : at, :], s_land[at : at + 1, :]
                )

    def share(src_of, to, n, peer_list):
        for _, ctx, chan, peer, ident in peer_list:
            remote(src_of(ctx, chan), rows_at(landed_ref, to, tiles), n, ident).start()
        own = pltpu.make_async_copy(src_of(my_ctx, my_chan), rows_at(landed_ref, to, tiles), own_sem.at[n - 3])
        own.start()
        return own

    conv_own = share(lambda ctx, chan: rows_at(conv, chan * blocks + ctx * tiles, tiles), me * 2 * tiles, 3, others)

    whole(c_stage, 2, peers - 1).wait_recv()
    for ch in range(n_merge):
        c_pad[ch * span : ch * span + blocks, :] = reverse(c_land[ch * blocks : (ch + 1) * blocks, :])
        for dd in range(STEPS):
            at = ch * span + dd
            c_lhs[ch, :, dd * LANES : (dd + 1) * LANES] = c_pad[at : at + blocks, :].astype(BF16)

    for g in range(blocks // STEPS):
        n = blocks - g * STEPS
        for ch in range(n_merge):
            part = jnp.dot(c_lhs[ch, g * STEPS : blocks, :], band(1 + ch, g), preferred_element_type=F32)
            corr[0:n, :] = part if g == 0 and ch == 0 else corr[0:n, :] + part
    corr[...] = reverse(corr[...]) * scale
    corr_rows = peers * 2 * tiles
    corr_own = share(
        lambda ctx, chan: rows_at(corr, ctx * tiles, tiles),
        corr_rows + my_chan * blocks + my_ctx * tiles, 4, [o for o in others if o[0]],
    )

    for g in range(blocks // STEPS):
        n = blocks - g * STEPS
        lhs = jnp.concatenate([c_lhs[ch, g * STEPS : blocks, :] for ch in range(n_merge)], axis=0)
        prod = jnp.dot(lhs, band(0, g), preferred_element_type=F32)
        for ch in range(n_merge):
            part = prod[ch * n : (ch + 1) * n]
            rows = slice(ch * blocks, ch * blocks + n)
            back[rows, :] = part if g == 0 else back[rows, :] + part
    back[...] = reverse(back[...])
    back_own = share(
        lambda ctx, chan: rows_at(back, chan * blocks + ctx * tiles, tiles), (me * 2 + 1) * tiles, 5, others
    )

    corr_own.wait()
    whole(f_stage, 4, n_ctx - 1).wait_recv()
    held = rows_at(landed_ref, corr_rows + my_chan * blocks, blocks)
    for j in range(1, n_merge):
        remote(held, held, 6, {"ctx": my_ctx, "chan": (my_chan + j) % n_merge}).start()

    whole(f_stage, 0, n_ctx - 1).wait_send()
    whole(s_stage, 1, peers - 1).wait_send()
    whole(c_stage, 2, peers - 1).wait_send()
    conv_own.wait()
    back_own.wait()
    whole(s_stage, 3, peers - 1).wait_send()
    whole(f_stage, 4, n_ctx - 1).wait_send()
    whole(s_stage, 5, peers - 1).wait_send()
    whole(s_stage, 3, peers - 1).wait_recv()
    if n_merge > 1:
        whole(s_stage, 6, (n_merge - 1) * n_ctx).wait_send()
        whole(s_stage, 6, (n_merge - 1) * n_ctx).wait_recv()
    whole(s_stage, 5, peers - 1).wait_recv()


def gate_kernel(go_ref, k_ref, v_ref, landed_ref, dq_ref, dk_ref, dv_ref, df_ref):
    rows, width = go_ref.shape
    tiles = width // LANES
    for k in range(tiles):
        cols = slice(k * LANES, (k + 1) * LANES)
        conv = landed_ref[pl.ds(k, rows, stride=2 * tiles), :]
        back = landed_ref[pl.ds(tiles + k, rows, stride=2 * tiles), :]
        dq_ref[:, cols] = (go_ref[:, cols].astype(F32) * conv).astype(BF16)
        dk_ref[:, cols] = (back * v_ref[:, cols].astype(F32)).astype(BF16)
        dv_ref[:, cols] = (back * k_ref[:, cols].astype(F32)).astype(BF16)
        df_ref[:, cols] = landed_ref[pl.ds(rows * 2 * tiles + k, rows, stride=tiles), :]


def vmem(count):
    return [pl.BlockSpec(memory_space=pltpu.VMEM)] * count


def local(grad_out, query, key_proj, value, filter_param):
    n_ctx = lax.axis_size("ctx")
    n_chan = lax.axis_size("chan")
    rows, width = grad_out.shape
    tiles = width // LANES
    n_merge = n_chan if rows == n_ctx * n_chan else 1
    peers = n_ctx * n_merge
    blocks = n_ctx * tiles
    if rows != peers or filter_param.shape[0] != rows or tiles % 8 or blocks % STEPS:
        raise ValueError("unsupported sizes")
    scale = 1.0 / math.sqrt(n_ctx * width)
    span = blocks + STEPS
    dma = pltpu.SemaphoreType.DMA

    def buffer(*shape, dtype=F32):
        return pltpu.VMEM(shape, dtype)

    landed = pl.pallas_call(
        functools.partial(convolve_kernel, n_ctx, n_merge, scale),
        out_shape=jax.ShapeDtypeStruct((peers * 3 * tiles, LANES), F32),
        in_specs=[pl.BlockSpec(memory_space=pl.ANY)] * 5,
        out_specs=pl.BlockSpec(memory_space=pl.ANY),
        scratch_shapes=[
            buffer(rows, width, dtype=BF16),
            buffer(rows, width, dtype=BF16),
            buffer(rows, width, dtype=BF16),
            buffer(rows, width, dtype=BF16),
            buffer(rows, width),
            dma((5,)),
            buffer(rows * tiles, LANES),
            buffer(rows * tiles, LANES),
            buffer(rows * tiles, LANES),
            buffer(blocks, LANES),
            buffer(n_merge * span, LANES),
            buffer(n_merge * blocks, LANES),
            buffer(n_merge * span, LANES),
            buffer(n_merge, blocks, DEPTH, dtype=BF16),
            buffer(n_merge, blocks, DEPTH, dtype=BF16),
            buffer(1 + n_merge, blocks * LANES, LANES, dtype=BF16),
            buffer(n_merge * blocks, LANES),
            buffer(n_merge * blocks, LANES),
            buffer(blocks, LANES),
            dma((7,)),
            dma((7,)),
            dma((3,)),
        ],
        compiler_params=pltpu.CompilerParams(
            collective_id=0, has_side_effects=True, vmem_limit_bytes=VMEM_BYTES
        ),
        name="long_convolutions",
    )(grad_out, query, key_proj, value, filter_param)
    dq, dk, dv, df = pl.pallas_call(
        gate_kernel,
        out_shape=(
            jax.ShapeDtypeStruct((rows, width), BF16),
            jax.ShapeDtypeStruct((rows, width), BF16),
            jax.ShapeDtypeStruct((rows, width), BF16),
            jax.ShapeDtypeStruct((rows, width), F32),
        ),
        in_specs=vmem(4),
        out_specs=tuple(vmem(4)),
        compiler_params=pltpu.CompilerParams(vmem_limit_bytes=VMEM_BYTES),
        name="gate_gradients",
    )(grad_out, key_proj, value, landed)
    if n_merge == 1:
        df = lax.psum(df, "chan")
    return (dq, dk, dv, df)


def solution(mesh):
    in_specs = (
        P("chan", "ctx"),
        P("chan", "ctx"),
        P("chan", "ctx"),
        P("chan", "ctx"),
        P(None, "ctx"),
    )
    out_specs = (P("chan", "ctx"), P("chan", "ctx"), P("chan", "ctx"), P(None, "ctx"))
    return jax.shard_map(local, mesh=mesh, in_specs=in_specs, out_specs=out_specs, check_vma=False)
```

```python
import functools
import math

import jax
import jax.numpy as jnp
from jax import lax
from jax.experimental import pallas as pl
from jax.experimental.pallas import tpu as pltpu
from jax.sharding import PartitionSpec as P

LANES = 128
STEPS = 16
VMEM_BYTES = 60 * 1024 * 1024
DEPTH = STEPS * LANES
F32 = jnp.float32
BF16 = jnp.bfloat16


def rows_at(ref, start, count):
    return ref.at[pl.ds(pl.multiple_of(start, 8), count), :]


def split_rows(values, stage, tiles):
    for k in range(tiles):
        stage[pl.ds(k, values.shape[0], stride=tiles), :] = values[:, k * LANES : (k + 1) * LANES]


def convolve_kernel(n_ctx, n_merge, scale, go_hbm, q_hbm, k_hbm, v_hbm, f_hbm, landed_ref,
                    go_ref, q_ref, k_ref, v_ref, f_ref, load_sem, f_stage, s_stage, c_stage, f_land, s_land, c_land, c_pad, s_lhs, c_lhs, toep,
                    conv, back, corr, send_sem, recv_sem, own_sem):
    loads = [
        pltpu.make_async_copy(src, dst, load_sem.at[n])
        for n, (src, dst) in enumerate(
            [(f_hbm, f_ref), (k_hbm, k_ref), (v_hbm, v_ref), (go_hbm, go_ref), (q_hbm, q_ref)]
        )
    ]
    for load in loads:
        load.start()
    tiles = go_ref.shape[1] // LANES
    blocks = n_ctx * tiles
    span = blocks + STEPS
    peers = n_ctx * n_merge
    my_ctx = lax.axis_index("ctx")
    my_chan = lax.axis_index("chan") if n_merge > 1 else 0
    me = my_chan * n_ctx + my_ctx

    offsets = [(c, j) for c in range(n_ctx) for j in range(n_merge) if (c, j) != (0, 0)]
    offsets.sort(key=lambda o: (abs(o[0] - n_ctx // 2), o))
    others = []
    for c, j in offsets:
        ctx = (my_ctx + c) % n_ctx
        chan = (my_chan + j) % n_merge if n_merge > 1 else 0
        ident = {"ctx": ctx, "chan": chan} if n_merge > 1 else {"ctx": ctx}
        others.append((j == 0, ctx, chan, chan * n_ctx + ctx, ident))

    barrier = pltpu.get_barrier_semaphore()
    for _, _, _, _, ident in others:
        pl.semaphore_signal(barrier, inc=1, device_id=ident, device_id_type=pl.DeviceIdType.MESH)

    def remote(src, dst, n, ident):
        return pltpu.make_async_remote_copy(
            src_ref=src, dst_ref=dst, send_sem=send_sem.at[n], recv_sem=recv_sem.at[n],
            device_id=ident, device_id_type=pl.DeviceIdType.MESH,
        )

    def whole(stage, n, count):
        part = stage.at[pl.ds(0, count * tiles), :]
        return remote(part, part, n, others[0][4])

    loads[0].wait()
    split_rows(f_ref[...] * scale, f_stage, tiles)
    loads[1].wait()
    loads[2].wait()
    split_rows(k_ref[...].astype(F32) * v_ref[...].astype(F32), s_stage, tiles)
    pl.semaphore_wait(barrier, peers - 1)
    for same, ctx, chan, peer, ident in others:
        if same:
            remote(rows_at(f_stage, peer * tiles, tiles), rows_at(f_land, my_ctx * tiles, tiles), 0, ident).start()
    for _, ctx, chan, peer, ident in others:
        remote(
            rows_at(s_stage, peer * tiles, tiles),
            rows_at(s_land, my_chan * span + STEPS + my_ctx * tiles, tiles), 1, ident,
        ).start()
    loads[3].wait()
    loads[4].wait()
    split_rows(go_ref[...].astype(F32) * q_ref[...].astype(F32), c_stage, tiles)
    for _, ctx, chan, peer, ident in others:
        remote(
            rows_at(c_stage, peer * tiles, tiles),
            rows_at(c_land, my_chan * blocks + my_ctx * tiles, tiles), 2, ident,
        ).start()
    mine = pl.ds(pl.multiple_of(me * tiles, 8), tiles)
    f_land[pl.ds(pl.multiple_of(my_ctx * tiles, 8), tiles), :] = f_stage[mine, :]
    s_land[pl.ds(pl.multiple_of(my_chan * span + STEPS + my_ctx * tiles, 8), tiles), :] = s_stage[mine, :]
    c_land[pl.ds(pl.multiple_of(my_chan * blocks + my_ctx * tiles, 8), tiles), :] = c_stage[mine, :]
    for ch in range(n_merge):
        s_land[ch * span : ch * span + STEPS, :] = jnp.zeros((STEPS, LANES), F32)
        c_pad[ch * span + blocks : (ch + 1) * span, :] = jnp.zeros((STEPS, LANES), F32)

    flip = (
        lax.broadcasted_iota(jnp.int32, (LANES, LANES), 0) + lax.broadcasted_iota(jnp.int32, (LANES, LANES), 1)
        == LANES - 1
    ).astype(BF16)
    lane = lax.broadcasted_iota(jnp.int32, (8, LANES), 1)
    first_rows = lane < LANES - lax.broadcasted_iota(jnp.int32, (8, LANES), 0)

    def reverse(values):
        high = values.astype(BF16)
        out = jnp.dot(high, flip, preferred_element_type=F32)
        if values.dtype == F32:
            low = (values - high.astype(F32)).astype(BF16)
            out = out + jnp.dot(low, flip, preferred_element_type=F32)
        return out

    def skew(before, now):
        picked = jnp.where(first_rows, jnp.broadcast_to(now, (8, LANES)), jnp.broadcast_to(before, (8, LANES)))
        return pltpu.roll(picked, 0, 1, stride=1, stride_axis=0)

    def tile(left, here):
        parts = [here]
        for shift in range(8, LANES, 8):
            parts.append(pltpu.roll(jnp.where(lane < LANES - shift, here, left), shift, 1))
        return jnp.concatenate(parts, axis=0).astype(BF16)

    whole(f_stage, 0, n_ctx - 1).wait_recv()

    def build(src, carry):
        before, left = carry
        rows = f_land[pl.ds(pl.multiple_of(src * tiles, 8), tiles), :]
        for k in range(tiles):
            now = rows[k : k + 1, :]
            here = skew(before, now)
            toep[0, pl.ds(pl.multiple_of((src * tiles + k) * LANES, LANES), LANES), :] = tile(left, here)
            before, left = now, here
        return before, left

    lax.fori_loop(0, n_ctx, build, (jnp.zeros((1, LANES), F32), jnp.zeros((8, LANES), F32)))
    whole(s_stage, 1, peers - 1).wait_recv()
    for ch in range(n_merge):
        for dd in range(STEPS):
            at = ch * span + STEPS - dd
            s_lhs[ch, :, dd * LANES : (dd + 1) * LANES] = s_land[at : at + blocks, :].astype(BF16)
    lefts = [jnp.zeros((8, LANES), F32)] * n_merge

    def band(n, g):
        return toep[n, g * DEPTH : (g + 1) * DEPTH, :]

    for g in range(blocks // STEPS):
        n = blocks - g * STEPS
        lhs = jnp.concatenate([s_lhs[ch, 0:n, :] for ch in range(n_merge)], axis=0)
        prod = jnp.dot(lhs, band(0, g), preferred_element_type=F32)
        for ch in range(n_merge):
            part = prod[ch * n : (ch + 1) * n]
            rows = slice(ch * blocks + g * STEPS, (ch + 1) * blocks)
            conv[rows, :] = part if g == 0 else conv[rows, :] + part
            for block in range(g * STEPS, (g + 1) * STEPS):
                at = ch * span + STEPS + block
                here = skew(s_land[at - 1 : at, :], s_land[at : at + 1, :])
                toep[1 + ch, block * LANES : (block + 1) * LANES, :] = tile(lefts[ch], here)
                lefts[ch] = here

    def share(src_of, to, n, peer_list):
        for _, ctx, chan, peer, ident in peer_list:
            remote(src_of(ctx, chan), rows_at(landed_ref, to, tiles), n, ident).start()
        own = pltpu.make_async_copy(src_of(my_ctx, my_chan), rows_at(landed_ref, to, tiles), own_sem.at[n - 3])
        own.start()
        return own

    conv_own = share(lambda ctx, chan: rows_at(conv, chan * blocks + ctx * tiles, tiles), me * 2 * tiles, 3, others)

    whole(c_stage, 2, peers - 1).wait_recv()
    for ch in range(n_merge):
        c_pad[ch * span : ch * span + blocks, :] = reverse(c_land[ch * blocks : (ch + 1) * blocks, :].astype(BF16))
        for dd in range(STEPS):
            at = ch * span + dd
            c_lhs[ch, :, dd * LANES : (dd + 1) * LANES] = c_pad[at : at + blocks, :].astype(BF16)

    for g in range(blocks // STEPS):
        n = blocks - g * STEPS
        for ch in range(n_merge):
            part = jnp.dot(c_lhs[ch, g * STEPS : blocks, :], band(1 + ch, g), preferred_element_type=F32)
            corr[0:n, :] = part if g == 0 and ch == 0 else corr[0:n, :] + part
    corr[...] = reverse(corr[...]) * scale
    corr_rows = peers * 2 * tiles
    corr_own = share(
        lambda ctx, chan: rows_at(corr, ctx * tiles, tiles),
        corr_rows + my_chan * blocks + my_ctx * tiles, 4, [o for o in others if o[0]],
    )

    for g in range(blocks // STEPS):
        n = blocks - g * STEPS
        lhs = jnp.concatenate([c_lhs[ch, g * STEPS : blocks, :] for ch in range(n_merge)], axis=0)
        prod = jnp.dot(lhs, band(0, g), preferred_element_type=F32)
        for ch in range(n_merge):
            part = prod[ch * n : (ch + 1) * n]
            rows = slice(ch * blocks, ch * blocks + n)
            back[rows, :] = part if g == 0 else back[rows, :] + part
    back[...] = reverse(back[...])
    back_own = share(
        lambda ctx, chan: rows_at(back, chan * blocks + ctx * tiles, tiles), (me * 2 + 1) * tiles, 5, others
    )

    corr_own.wait()
    whole(f_stage, 4, n_ctx - 1).wait_recv()
    held = rows_at(landed_ref, corr_rows + my_chan * blocks, blocks)
    for j in range(1, n_merge):
        remote(held, held, 6, {"ctx": my_ctx, "chan": (my_chan + j) % n_merge}).start()

    whole(f_stage, 0, n_ctx - 1).wait_send()
    whole(s_stage, 1, peers - 1).wait_send()
    whole(c_stage, 2, peers - 1).wait_send()
    conv_own.wait()
    back_own.wait()
    whole(s_stage, 3, peers - 1).wait_send()
    whole(f_stage, 4, n_ctx - 1).wait_send()
    whole(s_stage, 5, peers - 1).wait_send()
    whole(s_stage, 3, peers - 1).wait_recv()
    if n_merge > 1:
        whole(s_stage, 6, (n_merge - 1) * n_ctx).wait_send()
        whole(s_stage, 6, (n_merge - 1) * n_ctx).wait_recv()
    whole(s_stage, 5, peers - 1).wait_recv()


def gate_kernel(go_ref, k_ref, v_ref, landed_ref, dq_ref, dk_ref, dv_ref, df_ref):
    rows, width = go_ref.shape
    tiles = width // LANES
    for k in range(tiles):
        cols = slice(k * LANES, (k + 1) * LANES)
        conv = landed_ref[pl.ds(k, rows, stride=2 * tiles), :]
        back = landed_ref[pl.ds(tiles + k, rows, stride=2 * tiles), :]
        dq_ref[:, cols] = (go_ref[:, cols].astype(F32) * conv).astype(BF16)
        dk_ref[:, cols] = (back * v_ref[:, cols].astype(F32)).astype(BF16)
        dv_ref[:, cols] = (back * k_ref[:, cols].astype(F32)).astype(BF16)
        df_ref[:, cols] = landed_ref[pl.ds(rows * 2 * tiles + k, rows, stride=tiles), :]


def vmem(count):
    return [pl.BlockSpec(memory_space=pltpu.VMEM)] * count


def local(grad_out, query, key_proj, value, filter_param):
    n_ctx = lax.axis_size("ctx")
    n_chan = lax.axis_size("chan")
    rows, width = grad_out.shape
    tiles = width // LANES
    n_merge = n_chan if rows == n_ctx * n_chan else 1
    peers = n_ctx * n_merge
    blocks = n_ctx * tiles
    if rows != peers or filter_param.shape[0] != rows or tiles % 8 or blocks % STEPS:
        raise ValueError("unsupported sizes")
    scale = 1.0 / math.sqrt(n_ctx * width)
    span = blocks + STEPS
    dma = pltpu.SemaphoreType.DMA

    def buffer(*shape, dtype=F32):
        return pltpu.VMEM(shape, dtype)

    landed = pl.pallas_call(
        functools.partial(convolve_kernel, n_ctx, n_merge, scale),
        out_shape=jax.ShapeDtypeStruct((peers * 3 * tiles, LANES), F32),
        in_specs=[pl.BlockSpec(memory_space=pl.ANY)] * 5,
        out_specs=pl.BlockSpec(memory_space=pl.ANY),
        scratch_shapes=[
            buffer(rows, width, dtype=BF16),
            buffer(rows, width, dtype=BF16),
            buffer(rows, width, dtype=BF16),
            buffer(rows, width, dtype=BF16),
            buffer(rows, width),
            dma((5,)),
            buffer(rows * tiles, LANES),
            buffer(rows * tiles, LANES),
            buffer(rows * tiles, LANES),
            buffer(blocks, LANES),
            buffer(n_merge * span, LANES),
            buffer(n_merge * blocks, LANES),
            buffer(n_merge * span, LANES),
            buffer(n_merge, blocks, DEPTH, dtype=BF16),
            buffer(n_merge, blocks, DEPTH, dtype=BF16),
            buffer(1 + n_merge, blocks * LANES, LANES, dtype=BF16),
            buffer(n_merge * blocks, LANES),
            buffer(n_merge * blocks, LANES),
            buffer(blocks, LANES),
            dma((7,)),
            dma((7,)),
            dma((3,)),
        ],
        compiler_params=pltpu.CompilerParams(
            collective_id=0, has_side_effects=True, vmem_limit_bytes=VMEM_BYTES
        ),
        name="long_convolutions",
    )(grad_out, query, key_proj, value, filter_param)
    dq, dk, dv, df = pl.pallas_call(
        gate_kernel,
        out_shape=(
            jax.ShapeDtypeStruct((rows, width), BF16),
            jax.ShapeDtypeStruct((rows, width), BF16),
            jax.ShapeDtypeStruct((rows, width), BF16),
            jax.ShapeDtypeStruct((rows, width), F32),
        ),
        in_specs=vmem(4),
        out_specs=tuple(vmem(4)),
        compiler_params=pltpu.CompilerParams(vmem_limit_bytes=VMEM_BYTES),
        name="gate_gradients",
    )(grad_out, key_proj, value, landed)
    if n_merge == 1:
        df = lax.psum(df, "chan")
    return (dq, dk, dv, df)


def solution(mesh):
    in_specs = (
        P("chan", "ctx"),
        P("chan", "ctx"),
        P("chan", "ctx"),
        P("chan", "ctx"),
        P(None, "ctx"),
    )
    out_specs = (P("chan", "ctx"), P("chan", "ctx"), P("chan", "ctx"), P(None, "ctx"))
    return jax.shard_map(local, mesh=mesh, in_specs=in_specs, out_specs=out_specs, check_vma=False)
```

```python
import functools
import math

import jax
import jax.numpy as jnp
from jax import lax
from jax.experimental import pallas as pl
from jax.experimental.pallas import tpu as pltpu
from jax.sharding import PartitionSpec as P

LANES = 128
STEPS = 16
VMEM_BYTES = 60 * 1024 * 1024
DEPTH = STEPS * LANES
F32 = jnp.float32
BF16 = jnp.bfloat16


def rows_at(ref, start, count):
    return ref.at[pl.ds(pl.multiple_of(start, 8), count), :]


def split_rows(values, stage, tiles):
    for k in range(tiles):
        stage[pl.ds(k, values.shape[0], stride=tiles), :] = values[:, k * LANES : (k + 1) * LANES]


def convolve_kernel(n_ctx, n_merge, scale, go_hbm, q_hbm, k_hbm, v_hbm, f_hbm, landed_ref,
                    go_ref, q_ref, k_ref, v_ref, f_ref, load_sem, f_stage, s_stage, c_stage, f_land, s_land, c_land, c_pad, s_lhs, c_lhs, toep, gram, partial,
                    conv, back, corr, send_sem, recv_sem, own_sem):
    loads = [
        pltpu.make_async_copy(src, dst, load_sem.at[n])
        for n, (src, dst) in enumerate(
            [(f_hbm, f_ref), (k_hbm, k_ref), (v_hbm, v_ref), (go_hbm, go_ref), (q_hbm, q_ref)]
        )
    ]
    for load in loads:
        load.start()
    tiles = go_ref.shape[1] // LANES
    blocks = n_ctx * tiles
    span = blocks + STEPS
    peers = n_ctx * n_merge
    my_ctx = lax.axis_index("ctx")
    my_chan = lax.axis_index("chan") if n_merge > 1 else 0
    me = my_chan * n_ctx + my_ctx

    offsets = [(c, j) for c in range(n_ctx) for j in range(n_merge) if (c, j) != (0, 0)]
    offsets.sort(key=lambda o: (abs(o[0] - n_ctx // 2), o))
    others = []
    for c, j in offsets:
        ctx = (my_ctx + c) % n_ctx
        chan = (my_chan + j) % n_merge if n_merge > 1 else 0
        ident = {"ctx": ctx, "chan": chan} if n_merge > 1 else {"ctx": ctx}
        others.append((j == 0, ctx, chan, chan * n_ctx + ctx, ident))

    barrier = pltpu.get_barrier_semaphore()
    for _, _, _, _, ident in others:
        pl.semaphore_signal(barrier, inc=1, device_id=ident, device_id_type=pl.DeviceIdType.MESH)

    def remote(src, dst, n, ident):
        return pltpu.make_async_remote_copy(
            src_ref=src, dst_ref=dst, send_sem=send_sem.at[n], recv_sem=recv_sem.at[n],
            device_id=ident, device_id_type=pl.DeviceIdType.MESH,
        )

    def whole(stage, n, count):
        part = stage.at[pl.ds(0, count * tiles), :]
        return remote(part, part, n, others[0][4])

    loads[0].wait()
    split_rows(f_ref[...] * scale, f_stage, tiles)
    loads[1].wait()
    loads[2].wait()
    split_rows(k_ref[...].astype(F32) * v_ref[...].astype(F32), s_stage, tiles)
    pl.semaphore_wait(barrier, peers - 1)
    for same, ctx, chan, peer, ident in others:
        if same:
            remote(rows_at(f_stage, peer * tiles, tiles), rows_at(f_land, my_ctx * tiles, tiles), 0, ident).start()
    for _, ctx, chan, peer, ident in others:
        remote(
            rows_at(s_stage, peer * tiles, tiles),
            rows_at(s_land, my_chan * span + STEPS + my_ctx * tiles, tiles), 1, ident,
        ).start()
    loads[3].wait()
    loads[4].wait()
    split_rows(go_ref[...].astype(F32) * q_ref[...].astype(F32), c_stage, tiles)
    for _, ctx, chan, peer, ident in others:
        remote(
            rows_at(c_stage, peer * tiles, tiles),
            rows_at(c_land, my_chan * blocks + my_ctx * tiles, tiles), 2, ident,
        ).start()
    mine = pl.ds(pl.multiple_of(me * tiles, 8), tiles)
    f_land[pl.ds(pl.multiple_of(my_ctx * tiles, 8), tiles), :] = f_stage[mine, :]
    s_land[pl.ds(pl.multiple_of(my_chan * span + STEPS + my_ctx * tiles, 8), tiles), :] = s_stage[mine, :]
    c_land[pl.ds(pl.multiple_of(my_chan * blocks + my_ctx * tiles, 8), tiles), :] = c_stage[mine, :]
    gram[:, blocks * LANES : (blocks + 1) * LANES] = jnp.zeros((LANES, LANES), F32)
    for ch in range(n_merge):
        s_land[ch * span : ch * span + STEPS, :] = jnp.zeros((STEPS, LANES), F32)
        c_pad[ch * span + blocks : (ch + 1) * span, :] = jnp.zeros((STEPS, LANES), F32)

    lane = lax.broadcasted_iota(jnp.int32, (LANES, LANES), 1)
    row = lax.broadcasted_iota(jnp.int32, (LANES, LANES), 0)
    flip = (lane + row == LANES - 1).astype(BF16)
    current = lane < LANES - row

    def reverse(values):
        high = values.astype(BF16)
        out = jnp.dot(high, flip, preferred_element_type=F32)
        if values.dtype == F32:
            low = (values - high.astype(F32)).astype(BF16)
            out = out + jnp.dot(low, flip, preferred_element_type=F32)
        return out

    def skew(before, now):
        picked = jnp.where(
            current, jnp.broadcast_to(now, (LANES, LANES)), jnp.broadcast_to(before, (LANES, LANES))
        )
        return pltpu.roll(picked, 0, 1, stride=1, stride_axis=0).astype(BF16)

    whole(f_stage, 0, n_ctx - 1).wait_recv()

    def build(src, before):
        rows = f_land[pl.ds(pl.multiple_of(src * tiles, 8), tiles), :]
        for k in range(tiles):
            now = rows[k : k + 1, :]
            toep[pl.ds(pl.multiple_of((src * tiles + k) * LANES, LANES), LANES), :] = skew(before, now)
            before = now
        return before

    lax.fori_loop(0, n_ctx, build, jnp.zeros((1, LANES), F32))
    whole(s_stage, 1, peers - 1).wait_recv()
    ahead = blocks - STEPS
    for ch in range(n_merge):
        s_lhs[ch, 0:ahead, :] = jnp.zeros((ahead, DEPTH), BF16)
        for dd in range(STEPS):
            at = ch * span + STEPS - dd
            s_lhs[ch, ahead : ahead + blocks, dd * LANES : (dd + 1) * LANES] = s_land[at : at + blocks, :].astype(BF16)

    def band(g):
        return toep[g * DEPTH : (g + 1) * DEPTH, :]

    for g in range(blocks // STEPS):
        n = blocks - g * STEPS
        lhs = jnp.concatenate([s_lhs[ch, ahead : ahead + n, :] for ch in range(n_merge)], axis=0)
        prod = jnp.dot(lhs, band(g), preferred_element_type=F32)
        for ch in range(n_merge):
            part = prod[ch * n : (ch + 1) * n]
            rows = slice(ch * blocks + g * STEPS, (ch + 1) * blocks)
            conv[rows, :] = part if g == 0 else conv[rows, :] + part

    def share(src_of, to, n, peer_list):
        for _, ctx, chan, peer, ident in peer_list:
            remote(src_of(ctx, chan), rows_at(landed_ref, to, tiles), n, ident).start()
        own = pltpu.make_async_copy(src_of(my_ctx, my_chan), rows_at(landed_ref, to, tiles), own_sem.at[n - 3])
        own.start()
        return own

    conv_own = share(lambda ctx, chan: rows_at(conv, chan * blocks + ctx * tiles, tiles), me * 2 * tiles, 3, others)

    whole(c_stage, 2, peers - 1).wait_recv()
    for ch in range(n_merge):
        c_pad[ch * span : ch * span + blocks, :] = reverse(c_land[ch * blocks : (ch + 1) * blocks, :])
        for dd in range(STEPS):
            at = ch * span + dd
            c_lhs[ch, :, dd * LANES : (dd + 1) * LANES] = c_pad[at : at + blocks, :].astype(BF16)

    turned = jnp.concatenate(
        [c_pad[ch * span : ch * span + blocks, :].T for ch in range(n_merge)], axis=1
    ).astype(BF16)
    for g in range(blocks // STEPS):
        at = ahead - g * STEPS
        rhs = jnp.concatenate([s_lhs[ch, at : at + blocks, :] for ch in range(n_merge)], axis=0)
        gram[:, g * DEPTH : (g + 1) * DEPTH] = jnp.dot(turned, rhs, preferred_element_type=F32)

    for g in range(blocks // STEPS):
        n = blocks - g * STEPS
        lhs = jnp.concatenate([c_lhs[ch, g * STEPS : blocks, :] for ch in range(n_merge)], axis=0)
        prod = jnp.dot(lhs, band(g), preferred_element_type=F32)
        for ch in range(n_merge):
            part = prod[ch * n : (ch + 1) * n]
            rows = slice(ch * blocks, ch * blocks + n)
            back[rows, :] = part if g == 0 else back[rows, :] + part
        for e in range(g * STEPS, (g + 1) * STEPS):
            here = gram[:, e * LANES : (e + 1) * LANES]
            later = gram[:, (e + 1) * LANES : (e + 2) * LANES]
            turn = pltpu.roll(jnp.where(current, here, later), 0, 1, stride=1, stride_axis=0)
            partial[e * 8 : (e + 1) * 8, :] = jnp.sum(turn.reshape(LANES // 8, 8, LANES), axis=0)
    back[...] = reverse(back[...])
    back_own = share(
        lambda ctx, chan: rows_at(back, chan * blocks + ctx * tiles, tiles), (me * 2 + 1) * tiles, 5, others
    )
    total = partial[pl.ds(0, blocks, stride=8), :]
    for k in range(1, 8):
        total = total + partial[pl.ds(k, blocks, stride=8), :]
    corr[...] = reverse(total) * scale
    corr_own = share(
        lambda ctx, chan: rows_at(corr, ctx * tiles, tiles), peers * 2 * tiles + me * tiles, 4, others
    )

    whole(f_stage, 0, n_ctx - 1).wait_send()
    whole(s_stage, 1, peers - 1).wait_send()
    whole(c_stage, 2, peers - 1).wait_send()
    for own in (conv_own, back_own, corr_own):
        own.wait()
    for n in (3, 5, 4):
        whole(s_stage, n, peers - 1).wait_send()
        whole(s_stage, n, peers - 1).wait_recv()


def gate_kernel(go_ref, k_ref, v_ref, landed_ref, dq_ref, dk_ref, dv_ref, df_ref):
    rows, width = go_ref.shape
    tiles = width // LANES
    for k in range(tiles):
        cols = slice(k * LANES, (k + 1) * LANES)
        conv = landed_ref[pl.ds(k, rows, stride=2 * tiles), :]
        back = landed_ref[pl.ds(tiles + k, rows, stride=2 * tiles), :]
        dq_ref[:, cols] = (go_ref[:, cols].astype(F32) * conv).astype(BF16)
        dk_ref[:, cols] = (back * v_ref[:, cols].astype(F32)).astype(BF16)
        dv_ref[:, cols] = (back * k_ref[:, cols].astype(F32)).astype(BF16)
        df_ref[:, cols] = landed_ref[pl.ds(rows * 2 * tiles + k, rows, stride=tiles), :]


def vmem(count):
    return [pl.BlockSpec(memory_space=pltpu.VMEM)] * count


def local(grad_out, query, key_proj, value, filter_param):
    n_ctx = lax.axis_size("ctx")
    n_chan = lax.axis_size("chan")
    rows, width = grad_out.shape
    tiles = width // LANES
    n_merge = n_chan if rows == n_ctx * n_chan else 1
    peers = n_ctx * n_merge
    blocks = n_ctx * tiles
    if rows != peers or filter_param.shape[0] != rows or tiles % 8 or blocks % STEPS:
        raise ValueError("unsupported sizes")
    scale = 1.0 / math.sqrt(n_ctx * width)
    span = blocks + STEPS
    dma = pltpu.SemaphoreType.DMA

    def buffer(*shape, dtype=F32):
        return pltpu.VMEM(shape, dtype)

    landed = pl.pallas_call(
        functools.partial(convolve_kernel, n_ctx, n_merge, scale),
        out_shape=jax.ShapeDtypeStruct((peers * 3 * tiles, LANES), F32),
        in_specs=[pl.BlockSpec(memory_space=pl.ANY)] * 5,
        out_specs=pl.BlockSpec(memory_space=pl.ANY),
        scratch_shapes=[
            buffer(rows, width, dtype=BF16),
            buffer(rows, width, dtype=BF16),
            buffer(rows, width, dtype=BF16),
            buffer(rows, width, dtype=BF16),
            buffer(rows, width),
            dma((5,)),
            buffer(rows * tiles, LANES),
            buffer(rows * tiles, LANES),
            buffer(rows * tiles, LANES),
            buffer(blocks, LANES),
            buffer(n_merge * span, LANES),
            buffer(n_merge * blocks, LANES),
            buffer(n_merge * span, LANES),
            buffer(n_merge, 2 * blocks - STEPS, DEPTH, dtype=BF16),
            buffer(n_merge, blocks, DEPTH, dtype=BF16),
            buffer(blocks * LANES, LANES, dtype=BF16),
            buffer(LANES, (blocks + 1) * LANES),
            buffer(blocks * 8, LANES),
            buffer(n_merge * blocks, LANES),
            buffer(n_merge * blocks, LANES),
            buffer(blocks, LANES),
            dma((6,)),
            dma((6,)),
            dma((3,)),
        ],
        compiler_params=pltpu.CompilerParams(
            collective_id=0, has_side_effects=True, vmem_limit_bytes=VMEM_BYTES
        ),
        name="long_convolutions",
    )(grad_out, query, key_proj, value, filter_param)
    dq, dk, dv, df = pl.pallas_call(
        gate_kernel,
        out_shape=(
            jax.ShapeDtypeStruct((rows, width), BF16),
            jax.ShapeDtypeStruct((rows, width), BF16),
            jax.ShapeDtypeStruct((rows, width), BF16),
            jax.ShapeDtypeStruct((rows, width), F32),
        ),
        in_specs=vmem(4),
        out_specs=tuple(vmem(4)),
        compiler_params=pltpu.CompilerParams(vmem_limit_bytes=VMEM_BYTES),
        name="gate_gradients",
    )(grad_out, key_proj, value, landed)
    if n_merge == 1:
        df = lax.psum(df, "chan")
    return (dq, dk, dv, df)


def solution(mesh):
    in_specs = (
        P("chan", "ctx"),
        P("chan", "ctx"),
        P("chan", "ctx"),
        P("chan", "ctx"),
        P(None, "ctx"),
    )
    out_specs = (P("chan", "ctx"), P("chan", "ctx"), P("chan", "ctx"), P(None, "ctx"))
    return jax.shard_map(local, mesh=mesh, in_specs=in_specs, out_specs=out_specs, check_vma=False)
```

```python
import functools
import math

import jax
import jax.numpy as jnp
from jax import lax
from jax.experimental import pallas as pl
from jax.experimental.pallas import tpu as pltpu
from jax.sharding import PartitionSpec as P

LANES = 128
STEPS = 16
VMEM_BYTES = 60 * 1024 * 1024
DEPTH = STEPS * LANES
F32 = jnp.float32
BF16 = jnp.bfloat16


def rows_at(ref, start, count):
    return ref.at[pl.ds(pl.multiple_of(start, 8), count), :]


def split_rows(values, stage, tiles):
    for k in range(tiles):
        stage[pl.ds(k, values.shape[0], stride=tiles), :] = values[:, k * LANES : (k + 1) * LANES]


def convolve_kernel(n_ctx, n_merge, scale, go_hbm, q_hbm, k_hbm, v_hbm, f_hbm, landed_ref,
                    go_ref, q_ref, k_ref, v_ref, f_ref, load_sem, f_stage, s_stage, c_stage, f_land, s_land, c_land, c_pad, s_lhs, c_lhs, toep, gram, partial,
                    conv, back, corr, send_sem, recv_sem, own_sem):
    loads = [
        pltpu.make_async_copy(src, dst, load_sem.at[n])
        for n, (src, dst) in enumerate(
            [(f_hbm, f_ref), (k_hbm, k_ref), (v_hbm, v_ref), (go_hbm, go_ref), (q_hbm, q_ref)]
        )
    ]
    for load in loads:
        load.start()
    tiles = go_ref.shape[1] // LANES
    blocks = n_ctx * tiles
    span = blocks + STEPS
    peers = n_ctx * n_merge
    my_ctx = lax.axis_index("ctx")
    my_chan = lax.axis_index("chan") if n_merge > 1 else 0
    me = my_chan * n_ctx + my_ctx

    offsets = [(c, j) for c in range(n_ctx) for j in range(n_merge) if (c, j) != (0, 0)]
    offsets.sort(key=lambda o: (abs(o[0] - n_ctx // 2), o))
    others = []
    for c, j in offsets:
        ctx = (my_ctx + c) % n_ctx
        chan = (my_chan + j) % n_merge if n_merge > 1 else 0
        ident = {"ctx": ctx, "chan": chan} if n_merge > 1 else {"ctx": ctx}
        others.append((j == 0, ctx, chan, chan * n_ctx + ctx, ident))

    barrier = pltpu.get_barrier_semaphore()
    for _, _, _, _, ident in others:
        pl.semaphore_signal(barrier, inc=1, device_id=ident, device_id_type=pl.DeviceIdType.MESH)

    def remote(src, dst, n, ident):
        return pltpu.make_async_remote_copy(
            src_ref=src, dst_ref=dst, send_sem=send_sem.at[n], recv_sem=recv_sem.at[n],
            device_id=ident, device_id_type=pl.DeviceIdType.MESH,
        )

    def whole(stage, n, count):
        part = stage.at[pl.ds(0, count * tiles), :]
        return remote(part, part, n, others[0][4])

    loads[0].wait()
    split_rows(f_ref[...] * scale, f_stage, tiles)
    loads[1].wait()
    loads[2].wait()
    split_rows(k_ref[...].astype(F32) * v_ref[...].astype(F32), s_stage, tiles)
    loads[3].wait()
    loads[4].wait()
    split_rows(go_ref[...].astype(F32) * q_ref[...].astype(F32), c_stage, tiles)
    ahead = blocks - STEPS
    gram[:, blocks * LANES : (blocks + 1) * LANES] = jnp.zeros((LANES, LANES), F32)
    for ch in range(n_merge):
        s_land[ch * span : ch * span + STEPS, :] = jnp.zeros((STEPS, LANES), F32)
        c_pad[ch * span + blocks : (ch + 1) * span, :] = jnp.zeros((STEPS, LANES), F32)
        s_lhs[ch, 0:ahead, :] = jnp.zeros((ahead, DEPTH), BF16)
    pl.semaphore_wait(barrier, peers - 1)
    for same, ctx, chan, peer, ident in others:
        if same:
            remote(rows_at(f_stage, peer * tiles, tiles), rows_at(f_land, my_ctx * tiles, tiles), 0, ident).start()
    for _, ctx, chan, peer, ident in others:
        remote(
            rows_at(s_stage, peer * tiles, tiles),
            rows_at(s_land, my_chan * span + STEPS + my_ctx * tiles, tiles), 1, ident,
        ).start()
    for _, ctx, chan, peer, ident in others:
        remote(
            rows_at(c_stage, peer * tiles, tiles),
            rows_at(c_land, my_chan * blocks + my_ctx * tiles, tiles), 2, ident,
        ).start()
    mine = pl.ds(pl.multiple_of(me * tiles, 8), tiles)
    f_land[pl.ds(pl.multiple_of(my_ctx * tiles, 8), tiles), :] = f_stage[mine, :]
    s_land[pl.ds(pl.multiple_of(my_chan * span + STEPS + my_ctx * tiles, 8), tiles), :] = s_stage[mine, :]
    c_land[pl.ds(pl.multiple_of(my_chan * blocks + my_ctx * tiles, 8), tiles), :] = c_stage[mine, :]
    lane = lax.broadcasted_iota(jnp.int32, (LANES, LANES), 1)
    row = lax.broadcasted_iota(jnp.int32, (LANES, LANES), 0)
    flip = (lane + row == LANES - 1).astype(BF16)
    current = lane < LANES - row

    def reverse(values):
        high = values.astype(BF16)
        out = jnp.dot(high, flip, preferred_element_type=F32)
        if values.dtype == F32:
            low = (values - high.astype(F32)).astype(BF16)
            out = out + jnp.dot(low, flip, preferred_element_type=F32)
        return out

    def skew(before, now):
        picked = jnp.where(
            current, jnp.broadcast_to(now, (LANES, LANES)), jnp.broadcast_to(before, (LANES, LANES))
        )
        return pltpu.roll(picked, 0, 1, stride=1, stride_axis=0).astype(BF16)

    whole(f_stage, 0, n_ctx - 1).wait_recv()

    def build(src, before):
        rows = f_land[pl.ds(pl.multiple_of(src * tiles, 8), tiles), :]
        for k in range(tiles):
            now = rows[k : k + 1, :]
            toep[pl.ds(pl.multiple_of((src * tiles + k) * LANES, LANES), LANES), :] = skew(before, now)
            before = now
        return before

    lax.fori_loop(0, n_ctx, build, jnp.zeros((1, LANES), F32))
    whole(s_stage, 1, peers - 1).wait_recv()
    for ch in range(n_merge):
        for dd in range(STEPS):
            at = ch * span + STEPS - dd
            s_lhs[ch, ahead : ahead + blocks, dd * LANES : (dd + 1) * LANES] = s_land[at : at + blocks, :].astype(BF16)

    def band(g):
        return toep[g * DEPTH : (g + 1) * DEPTH, :]

    for g in range(blocks // STEPS):
        n = blocks - g * STEPS
        lhs = jnp.concatenate([s_lhs[ch, ahead : ahead + n, :] for ch in range(n_merge)], axis=0)
        prod = jnp.dot(lhs, band(g), preferred_element_type=F32)
        for ch in range(n_merge):
            part = prod[ch * n : (ch + 1) * n]
            rows = slice(ch * blocks + g * STEPS, (ch + 1) * blocks)
            conv[rows, :] = part if g == 0 else conv[rows, :] + part

    def share(src_of, to, n, peer_list):
        for _, ctx, chan, peer, ident in peer_list:
            remote(src_of(ctx, chan), rows_at(landed_ref, to, tiles), n, ident).start()
        own = pltpu.make_async_copy(src_of(my_ctx, my_chan), rows_at(landed_ref, to, tiles), own_sem.at[n - 3])
        own.start()
        return own

    conv_own = share(lambda ctx, chan: rows_at(conv, chan * blocks + ctx * tiles, tiles), me * 2 * tiles, 3, others)

    whole(c_stage, 2, peers - 1).wait_recv()
    for ch in range(n_merge):
        c_pad[ch * span : ch * span + blocks, :] = reverse(c_land[ch * blocks : (ch + 1) * blocks, :])
        for dd in range(STEPS):
            at = ch * span + dd
            c_lhs[ch, :, dd * LANES : (dd + 1) * LANES] = c_pad[at : at + blocks, :].astype(BF16)

    for g in range(blocks // STEPS):
        n = blocks - g * STEPS
        lhs = jnp.concatenate([c_lhs[ch, g * STEPS : blocks, :] for ch in range(n_merge)], axis=0)
        prod = jnp.dot(lhs, band(g), preferred_element_type=F32)
        for ch in range(n_merge):
            part = prod[ch * n : (ch + 1) * n]
            rows = slice(ch * blocks, ch * blocks + n)
            back[rows, :] = part if g == 0 else back[rows, :] + part
    back[...] = reverse(back[...])
    back_own = share(
        lambda ctx, chan: rows_at(back, chan * blocks + ctx * tiles, tiles), (me * 2 + 1) * tiles, 5, others
    )

    turned = jnp.concatenate(
        [c_pad[ch * span : ch * span + blocks, :].T for ch in range(n_merge)], axis=1
    ).astype(BF16)

    def diagonals(g):
        for e in range(g * STEPS, (g + 1) * STEPS):
            here = gram[:, e * LANES : (e + 1) * LANES]
            later = gram[:, (e + 1) * LANES : (e + 2) * LANES]
            turn = pltpu.roll(jnp.where(current, here, later), 0, 1, stride=1, stride_axis=0)
            partial[e * 8 : (e + 1) * 8, :] = jnp.sum(turn.reshape(LANES // 8, 8, LANES), axis=0)

    for g in range(blocks // STEPS):
        at = ahead - g * STEPS
        rhs = jnp.concatenate([s_lhs[ch, at : at + blocks, :] for ch in range(n_merge)], axis=0)
        gram[:, g * DEPTH : (g + 1) * DEPTH] = jnp.dot(turned, rhs, preferred_element_type=F32)
        if g > 0:
            diagonals(g - 1)
    diagonals(blocks // STEPS - 1)
    total = partial[pl.ds(0, blocks, stride=8), :]
    for k in range(1, 8):
        total = total + partial[pl.ds(k, blocks, stride=8), :]
    corr[...] = reverse(total) * scale
    corr_own = share(
        lambda ctx, chan: rows_at(corr, ctx * tiles, tiles), peers * 2 * tiles + me * tiles, 4, others
    )

    whole(f_stage, 0, n_ctx - 1).wait_send()
    whole(s_stage, 1, peers - 1).wait_send()
    whole(c_stage, 2, peers - 1).wait_send()
    for own in (conv_own, back_own, corr_own):
        own.wait()
    for n in (3, 5, 4):
        whole(s_stage, n, peers - 1).wait_send()
        whole(s_stage, n, peers - 1).wait_recv()


def gate_kernel(go_ref, k_ref, v_ref, landed_ref, dq_ref, dk_ref, dv_ref, df_ref):
    rows, width = go_ref.shape
    tiles = width // LANES
    for k in range(tiles):
        cols = slice(k * LANES, (k + 1) * LANES)
        conv = landed_ref[pl.ds(k, rows, stride=2 * tiles), :]
        back = landed_ref[pl.ds(tiles + k, rows, stride=2 * tiles), :]
        dq_ref[:, cols] = (go_ref[:, cols].astype(F32) * conv).astype(BF16)
        dk_ref[:, cols] = (back * v_ref[:, cols].astype(F32)).astype(BF16)
        dv_ref[:, cols] = (back * k_ref[:, cols].astype(F32)).astype(BF16)
        df_ref[:, cols] = landed_ref[pl.ds(rows * 2 * tiles + k, rows, stride=tiles), :]


def vmem(count):
    return [pl.BlockSpec(memory_space=pltpu.VMEM)] * count


def local(grad_out, query, key_proj, value, filter_param):
    n_ctx = lax.axis_size("ctx")
    n_chan = lax.axis_size("chan")
    rows, width = grad_out.shape
    tiles = width // LANES
    n_merge = n_chan if rows == n_ctx * n_chan else 1
    peers = n_ctx * n_merge
    blocks = n_ctx * tiles
    if rows != peers or filter_param.shape[0] != rows or tiles % 8 or blocks % STEPS:
        raise ValueError("unsupported sizes")
    scale = 1.0 / math.sqrt(n_ctx * width)
    span = blocks + STEPS
    dma = pltpu.SemaphoreType.DMA

    def buffer(*shape, dtype=F32):
        return pltpu.VMEM(shape, dtype)

    landed = pl.pallas_call(
        functools.partial(convolve_kernel, n_ctx, n_merge, scale),
        out_shape=jax.ShapeDtypeStruct((peers * 3 * tiles, LANES), F32),
        in_specs=[pl.BlockSpec(memory_space=pl.ANY)] * 5,
        out_specs=pl.BlockSpec(memory_space=pl.ANY),
        scratch_shapes=[
            buffer(rows, width, dtype=BF16),
            buffer(rows, width, dtype=BF16),
            buffer(rows, width, dtype=BF16),
            buffer(rows, width, dtype=BF16),
            buffer(rows, width),
            dma((5,)),
            buffer(rows * tiles, LANES),
            buffer(rows * tiles, LANES),
            buffer(rows * tiles, LANES),
            buffer(blocks, LANES),
            buffer(n_merge * span, LANES),
            buffer(n_merge * blocks, LANES),
            buffer(n_merge * span, LANES),
            buffer(n_merge, 2 * blocks - STEPS, DEPTH, dtype=BF16),
            buffer(n_merge, blocks, DEPTH, dtype=BF16),
            buffer(blocks * LANES, LANES, dtype=BF16),
            buffer(LANES, (blocks + 1) * LANES),
            buffer(blocks * 8, LANES),
            buffer(n_merge * blocks, LANES),
            buffer(n_merge * blocks, LANES),
            buffer(blocks, LANES),
            dma((6,)),
            dma((6,)),
            dma((3,)),
        ],
        compiler_params=pltpu.CompilerParams(
            collective_id=0, has_side_effects=True, vmem_limit_bytes=VMEM_BYTES
        ),
        name="long_convolutions",
    )(grad_out, query, key_proj, value, filter_param)
    dq, dk, dv, df = pl.pallas_call(
        gate_kernel,
        out_shape=(
            jax.ShapeDtypeStruct((rows, width), BF16),
            jax.ShapeDtypeStruct((rows, width), BF16),
            jax.ShapeDtypeStruct((rows, width), BF16),
            jax.ShapeDtypeStruct((rows, width), F32),
        ),
        in_specs=vmem(4),
        out_specs=tuple(vmem(4)),
        compiler_params=pltpu.CompilerParams(vmem_limit_bytes=VMEM_BYTES),
        name="gate_gradients",
    )(grad_out, key_proj, value, landed)
    if n_merge == 1:
        df = lax.psum(df, "chan")
    return (dq, dk, dv, df)


def solution(mesh):
    in_specs = (
        P("chan", "ctx"),
        P("chan", "ctx"),
        P("chan", "ctx"),
        P("chan", "ctx"),
        P(None, "ctx"),
    )
    out_specs = (P("chan", "ctx"), P("chan", "ctx"), P("chan", "ctx"), P(None, "ctx"))
    return jax.shard_map(local, mesh=mesh, in_specs=in_specs, out_specs=out_specs, check_vma=False)
```

```python
import functools
import math

import jax
import jax.numpy as jnp
from jax import lax
from jax.experimental import pallas as pl
from jax.experimental.pallas import tpu as pltpu
from jax.sharding import PartitionSpec as P

LANES = 128
STEPS = 16
VMEM_BYTES = 60 * 1024 * 1024
DEPTH = STEPS * LANES
F32 = jnp.float32
BF16 = jnp.bfloat16


def rows_at(ref, start, count):
    return ref.at[pl.ds(pl.multiple_of(start, 8), count), :]


def split_rows(values, stage, tiles):
    for k in range(tiles):
        stage[pl.ds(k, values.shape[0], stride=tiles), :] = values[:, k * LANES : (k + 1) * LANES]


def convolve_kernel(n_ctx, n_merge, scale, go_hbm, q_hbm, k_hbm, v_hbm, f_hbm, landed_ref,
                    go_ref, q_ref, k_ref, v_ref, f_ref, load_sem, f_stage, s_stage, c_stage, f_land, s_land, c_land, c_pad, s_lhs, c_lhs, toep, gram, partial,
                    conv, back, corr, send_sem, recv_sem, own_sem):
    loads = [
        pltpu.make_async_copy(src, dst, load_sem.at[n])
        for n, (src, dst) in enumerate(
            [(f_hbm, f_ref), (k_hbm, k_ref), (v_hbm, v_ref), (go_hbm, go_ref), (q_hbm, q_ref)]
        )
    ]
    for load in loads:
        load.start()
    tiles = go_ref.shape[1] // LANES
    blocks = n_ctx * tiles
    span = blocks + STEPS
    peers = n_ctx * n_merge
    my_ctx = lax.axis_index("ctx")
    my_chan = lax.axis_index("chan") if n_merge > 1 else 0
    me = my_chan * n_ctx + my_ctx

    offsets = [(c, j) for c in range(n_ctx) for j in range(n_merge) if (c, j) != (0, 0)]
    offsets.sort(key=lambda o: (abs(o[0] - n_ctx // 2), o))
    half = (len(offsets) + 1) // 2
    offsets = [o for k in range(half) for o in dict.fromkeys((offsets[k], offsets[len(offsets) - 1 - k]))]
    others = []
    for c, j in offsets:
        ctx = (my_ctx + c) % n_ctx
        chan = (my_chan + j) % n_merge if n_merge > 1 else 0
        ident = {"ctx": ctx, "chan": chan} if n_merge > 1 else {"ctx": ctx}
        others.append((j == 0, ctx, chan, chan * n_ctx + ctx, ident))

    barrier = pltpu.get_barrier_semaphore()
    for _, _, _, _, ident in others:
        pl.semaphore_signal(barrier, inc=1, device_id=ident, device_id_type=pl.DeviceIdType.MESH)

    def remote(src, dst, n, ident):
        return pltpu.make_async_remote_copy(
            src_ref=src, dst_ref=dst, send_sem=send_sem.at[n], recv_sem=recv_sem.at[n],
            device_id=ident, device_id_type=pl.DeviceIdType.MESH,
        )

    def whole(stage, n, count):
        part = stage.at[pl.ds(0, count * tiles), :]
        return remote(part, part, n, others[0][4])

    loads[0].wait()
    split_rows(f_ref[...] * scale, f_stage, tiles)
    loads[1].wait()
    loads[2].wait()
    split_rows(k_ref[...].astype(F32) * v_ref[...].astype(F32), s_stage, tiles)
    loads[3].wait()
    loads[4].wait()
    split_rows(go_ref[...].astype(F32) * q_ref[...].astype(F32), c_stage, tiles)
    ahead = blocks - STEPS
    gram[:, blocks * LANES : (blocks + 1) * LANES] = jnp.zeros((LANES, LANES), F32)
    for ch in range(n_merge):
        s_land[ch * span : ch * span + STEPS, :] = jnp.zeros((STEPS, LANES), F32)
        c_pad[ch * span + blocks : (ch + 1) * span, :] = jnp.zeros((STEPS, LANES), F32)
        s_lhs[ch, 0:ahead, :] = jnp.zeros((ahead, DEPTH), BF16)
    pl.semaphore_wait(barrier, peers - 1)
    for same, ctx, chan, peer, ident in others:
        if same:
            remote(rows_at(f_stage, peer * tiles, tiles), rows_at(f_land, my_ctx * tiles, tiles), 0, ident).start()
    for _, ctx, chan, peer, ident in others:
        remote(
            rows_at(s_stage, peer * tiles, tiles),
            rows_at(s_land, my_chan * span + STEPS + my_ctx * tiles, tiles), 1, ident,
        ).start()
    for _, ctx, chan, peer, ident in others:
        remote(
            rows_at(c_stage, peer * tiles, tiles),
            rows_at(c_land, my_chan * blocks + my_ctx * tiles, tiles), 2, ident,
        ).start()
    mine = pl.ds(pl.multiple_of(me * tiles, 8), tiles)
    f_land[pl.ds(pl.multiple_of(my_ctx * tiles, 8), tiles), :] = f_stage[mine, :]
    s_land[pl.ds(pl.multiple_of(my_chan * span + STEPS + my_ctx * tiles, 8), tiles), :] = s_stage[mine, :]
    c_land[pl.ds(pl.multiple_of(my_chan * blocks + my_ctx * tiles, 8), tiles), :] = c_stage[mine, :]
    lane = lax.broadcasted_iota(jnp.int32, (LANES, LANES), 1)
    row = lax.broadcasted_iota(jnp.int32, (LANES, LANES), 0)
    flip = (lane + row == LANES - 1).astype(BF16)
    current = lane < LANES - row

    def reverse(values):
        high = values.astype(BF16)
        out = jnp.dot(high, flip, preferred_element_type=F32)
        if values.dtype == F32:
            low = (values - high.astype(F32)).astype(BF16)
            out = out + jnp.dot(low, flip, preferred_element_type=F32)
        return out

    def skew(before, now):
        picked = jnp.where(
            current, jnp.broadcast_to(now, (LANES, LANES)), jnp.broadcast_to(before, (LANES, LANES))
        )
        return pltpu.roll(picked, 0, 1, stride=1, stride_axis=0).astype(BF16)

    whole(f_stage, 0, n_ctx - 1).wait_recv()

    def build(src, before):
        rows = f_land[pl.ds(pl.multiple_of(src * tiles, 8), tiles), :]
        for k in range(tiles):
            now = rows[k : k + 1, :]
            toep[pl.ds(pl.multiple_of((src * tiles + k) * LANES, LANES), LANES), :] = skew(before, now)
            before = now
        return before

    lax.fori_loop(0, n_ctx, build, jnp.zeros((1, LANES), F32))
    whole(s_stage, 1, peers - 1).wait_recv()
    for ch in range(n_merge):
        for dd in range(STEPS):
            at = ch * span + STEPS - dd
            s_lhs[ch, ahead : ahead + blocks, dd * LANES : (dd + 1) * LANES] = s_land[at : at + blocks, :].astype(BF16)

    def band(g):
        return toep[g * DEPTH : (g + 1) * DEPTH, :]

    for g in range(blocks // STEPS):
        n = blocks - g * STEPS
        lhs = jnp.concatenate([s_lhs[ch, ahead : ahead + n, :] for ch in range(n_merge)], axis=0)
        prod = jnp.dot(lhs, band(g), preferred_element_type=F32)
        for ch in range(n_merge):
            part = prod[ch * n : (ch + 1) * n]
            rows = slice(ch * blocks + g * STEPS, (ch + 1) * blocks)
            conv[rows, :] = part if g == 0 else conv[rows, :] + part

    def share(src_of, to, n, peer_list):
        for _, ctx, chan, peer, ident in peer_list:
            remote(src_of(ctx, chan), rows_at(landed_ref, to, tiles), n, ident).start()
        own = pltpu.make_async_copy(src_of(my_ctx, my_chan), rows_at(landed_ref, to, tiles), own_sem.at[n - 3])
        own.start()
        return own

    conv_own = share(lambda ctx, chan: rows_at(conv, chan * blocks + ctx * tiles, tiles), me * 2 * tiles, 3, others)

    whole(c_stage, 2, peers - 1).wait_recv()
    for ch in range(n_merge):
        c_pad[ch * span : ch * span + blocks, :] = reverse(c_land[ch * blocks : (ch + 1) * blocks, :])
        for dd in range(STEPS):
            at = ch * span + dd
            c_lhs[ch, :, dd * LANES : (dd + 1) * LANES] = c_pad[at : at + blocks, :].astype(BF16)

    for g in range(blocks // STEPS):
        n = blocks - g * STEPS
        lhs = jnp.concatenate([c_lhs[ch, g * STEPS : blocks, :] for ch in range(n_merge)], axis=0)
        prod = jnp.dot(lhs, band(g), preferred_element_type=F32)
        for ch in range(n_merge):
            part = prod[ch * n : (ch + 1) * n]
            rows = slice(ch * blocks, ch * blocks + n)
            back[rows, :] = part if g == 0 else back[rows, :] + part
    back[...] = reverse(back[...])
    back_own = share(
        lambda ctx, chan: rows_at(back, chan * blocks + ctx * tiles, tiles), (me * 2 + 1) * tiles, 5, others
    )

    turned = jnp.concatenate(
        [c_pad[ch * span : ch * span + blocks, :].T for ch in range(n_merge)], axis=1
    ).astype(BF16)

    def diagonals(g):
        for e in range(g * STEPS, (g + 1) * STEPS):
            here = gram[:, e * LANES : (e + 1) * LANES]
            later = gram[:, (e + 1) * LANES : (e + 2) * LANES]
            turn = pltpu.roll(jnp.where(current, here, later), 0, 1, stride=1, stride_axis=0)
            partial[e * 8 : (e + 1) * 8, :] = jnp.sum(turn.reshape(LANES // 8, 8, LANES), axis=0)

    for g in range(blocks // STEPS):
        at = ahead - g * STEPS
        rhs = jnp.concatenate([s_lhs[ch, at : at + blocks, :] for ch in range(n_merge)], axis=0)
        gram[:, g * DEPTH : (g + 1) * DEPTH] = jnp.dot(turned, rhs, preferred_element_type=F32)
        if g > 0:
            diagonals(g - 1)
    diagonals(blocks // STEPS - 1)
    total = partial[pl.ds(0, blocks, stride=8), :]
    for k in range(1, 8):
        total = total + partial[pl.ds(k, blocks, stride=8), :]
    corr[...] = reverse(total) * scale
    corr_own = share(
        lambda ctx, chan: rows_at(corr, ctx * tiles, tiles), peers * 2 * tiles + me * tiles, 4, others
    )

    whole(f_stage, 0, n_ctx - 1).wait_send()
    whole(s_stage, 1, peers - 1).wait_send()
    whole(c_stage, 2, peers - 1).wait_send()
    for own in (conv_own, back_own, corr_own):
        own.wait()
    for n in (3, 5, 4):
        whole(s_stage, n, peers - 1).wait_send()
        whole(s_stage, n, peers - 1).wait_recv()


def gate_kernel(go_ref, k_ref, v_ref, landed_ref, dq_ref, dk_ref, dv_ref, df_ref):
    rows, width = go_ref.shape
    tiles = width // LANES
    for k in range(tiles):
        cols = slice(k * LANES, (k + 1) * LANES)
        conv = landed_ref[pl.ds(k, rows, stride=2 * tiles), :]
        back = landed_ref[pl.ds(tiles + k, rows, stride=2 * tiles), :]
        dq_ref[:, cols] = (go_ref[:, cols].astype(F32) * conv).astype(BF16)
        dk_ref[:, cols] = (back * v_ref[:, cols].astype(F32)).astype(BF16)
        dv_ref[:, cols] = (back * k_ref[:, cols].astype(F32)).astype(BF16)
        df_ref[:, cols] = landed_ref[pl.ds(rows * 2 * tiles + k, rows, stride=tiles), :]


def vmem(count):
    return [pl.BlockSpec(memory_space=pltpu.VMEM)] * count


def local(grad_out, query, key_proj, value, filter_param):
    n_ctx = lax.axis_size("ctx")
    n_chan = lax.axis_size("chan")
    rows, width = grad_out.shape
    tiles = width // LANES
    n_merge = n_chan if rows == n_ctx * n_chan else 1
    peers = n_ctx * n_merge
    blocks = n_ctx * tiles
    if rows != peers or filter_param.shape[0] != rows or tiles % 8 or blocks % STEPS:
        raise ValueError("unsupported sizes")
    scale = 1.0 / math.sqrt(n_ctx * width)
    span = blocks + STEPS
    dma = pltpu.SemaphoreType.DMA

    def buffer(*shape, dtype=F32):
        return pltpu.VMEM(shape, dtype)

    landed = pl.pallas_call(
        functools.partial(convolve_kernel, n_ctx, n_merge, scale),
        out_shape=jax.ShapeDtypeStruct((peers * 3 * tiles, LANES), F32),
        in_specs=[pl.BlockSpec(memory_space=pl.ANY)] * 5,
        out_specs=pl.BlockSpec(memory_space=pl.ANY),
        scratch_shapes=[
            buffer(rows, width, dtype=BF16),
            buffer(rows, width, dtype=BF16),
            buffer(rows, width, dtype=BF16),
            buffer(rows, width, dtype=BF16),
            buffer(rows, width),
            dma((5,)),
            buffer(rows * tiles, LANES),
            buffer(rows * tiles, LANES),
            buffer(rows * tiles, LANES),
            buffer(blocks, LANES),
            buffer(n_merge * span, LANES),
            buffer(n_merge * blocks, LANES),
            buffer(n_merge * span, LANES),
            buffer(n_merge, 2 * blocks - STEPS, DEPTH, dtype=BF16),
            buffer(n_merge, blocks, DEPTH, dtype=BF16),
            buffer(blocks * LANES, LANES, dtype=BF16),
            buffer(LANES, (blocks + 1) * LANES),
            buffer(blocks * 8, LANES),
            buffer(n_merge * blocks, LANES),
            buffer(n_merge * blocks, LANES),
            buffer(blocks, LANES),
            dma((6,)),
            dma((6,)),
            dma((3,)),
        ],
        compiler_params=pltpu.CompilerParams(
            collective_id=0, has_side_effects=True, vmem_limit_bytes=VMEM_BYTES
        ),
        name="long_convolutions",
    )(grad_out, query, key_proj, value, filter_param)
    dq, dk, dv, df = pl.pallas_call(
        gate_kernel,
        out_shape=(
            jax.ShapeDtypeStruct((rows, width), BF16),
            jax.ShapeDtypeStruct((rows, width), BF16),
            jax.ShapeDtypeStruct((rows, width), BF16),
            jax.ShapeDtypeStruct((rows, width), F32),
        ),
        in_specs=vmem(4),
        out_specs=tuple(vmem(4)),
        compiler_params=pltpu.CompilerParams(vmem_limit_bytes=VMEM_BYTES),
        name="gate_gradients",
    )(grad_out, key_proj, value, landed)
    if n_merge == 1:
        df = lax.psum(df, "chan")
    return (dq, dk, dv, df)


def solution(mesh):
    in_specs = (
        P("chan", "ctx"),
        P("chan", "ctx"),
        P("chan", "ctx"),
        P("chan", "ctx"),
        P(None, "ctx"),
    )
    out_specs = (P("chan", "ctx"), P("chan", "ctx"), P("chan", "ctx"), P(None, "ctx"))
    return jax.shard_map(local, mesh=mesh, in_specs=in_specs, out_specs=out_specs, check_vma=False)
```
